512 devices in a mesh: ctx: 128 (over z, y, x_hi), tp: 4 (over x_lo, core).
Axes of the slice: x: 4 (x_hi: 2, x_lo: 2; x = x_hi * 2 + x_lo), y: 4, z: 16, core: 2. Of those that a mesh axis runs over, the one named last changes fastest.
Arguments:
- q_text: bfloat16 [16384, 3584], P('ctx', 'tp'), may hold values from -8 to 8, as said below
- kv_text: bfloat16 [16384, 1024], P('ctx', 'tp'), may hold values from -8 to 8, as said below
- patch_rows: bfloat16 [8192, 4608], P('ctx', 'tp'), may hold values from -6 to 6
- image_count: int32 [128], replicated, may hold values from 0 to 128, as said below
- w_out: bfloat16 [3584, 3584], P(('tp', 'ctx')), may hold values from -0.09375 to 0.09375
Outputs:
- layer_out: bfloat16 [16384, 3584], P('ctx', 'tp')
The draws below stay inside these ranges and needn't reach their ends.
Inputs may be any that keep to these rules, and one draw needn't show every extreme that they name: `image_count`: sums to 8192; at least one shard holds only image positions. `q_text`: rows at image positions are not read. `kv_text`: rows at image positions are not read.
All inputs are finite; a program needn't handle non-finite values.
Results may differ from the reference program's by a relative error of at most 0.015.
Values may be sent and summed in bfloat16 or wider, within the bound.
A program may use at most 128 MiB of HBM per device.

```python
import jax
import jax.numpy as jnp
from jax import lax

D = 3584
HQ = 28
KVH = 4
HD = 128
TOK_DEV = 128
LENGTH = 16384
IMG_DEV = 64
IMAGE_ROWS = 8192
N_CTX = 128


def draw_q_text(key, part):
    key = jax.random.fold_in(key, 1)
    base = jnp.clip(jax.random.normal(key, (LENGTH, D), dtype=jnp.float32), -6.0, 6.0)
    return base.astype(jnp.bfloat16)


def draw_kv_text(key, part):
    key = jax.random.fold_in(key, 2)
    base = jnp.clip(jax.random.normal(key, (LENGTH, KVH, 2, HD), dtype=jnp.float32), -6.0, 6.0)
    return base.reshape(LENGTH, 2 * KVH * HD).astype(jnp.bfloat16)


def draw_image_count(key, part):
    key = jax.random.fold_in(key, 7)
    lower = jax.random.randint(jax.random.fold_in(key, 1), (N_CTX // 2,), 0, TOK_DEV + 1)
    lower = lower.at[0].set(TOK_DEV)
    both = jnp.concatenate([lower, TOK_DEV - lower])
    order = jax.random.permutation(jax.random.fold_in(key, 2), N_CTX)
    return both[order].astype(jnp.int32)


def shard_levels(rng, shape, pieces, least, high):
    def one(dim, parts):
        steps = jax.random.uniform(jax.random.fold_in(jax.random.fold_in(rng, 6), dim), (parts,), jnp.float32, least / len(pieces), high / len(pieces))
        return jnp.repeat(jnp.exp(steps), shape[dim] // parts).reshape((-1,) + (1,) * (len(shape) - dim - 1))

    loudness = one(*pieces[0])
    for cut in pieces[1:]:
        loudness = loudness * one(*cut)
    return loudness


def gaussian(key, dims, width, bound, shards=(), held_as=jnp.bfloat16):
    array = jax.random.normal(key, dims, jnp.float32) * width
    if len(shards) > 0:
        array = shard_levels(key, dims, shards, -0.22, 0.18) * array
    return jnp.clip(array, min=-bound, max=bound).astype(held_as)


def setup_inputs(seed: int = 0) -> dict:
    splits = jax.random.split(jax.random.key(seed), 6)
    return {
        "q_text": draw_q_text(jax.random.fold_in(splits[5], 71), 0),
        "kv_text": draw_kv_text(jax.random.fold_in(splits[5], 71), 0),
        "patch_rows": gaussian(splits[2], (IMAGE_ROWS, (HQ + 2 * KVH) * HD), 1.0, 6.0, ((0, 128), (1, 4))),
        "image_count": draw_image_count(jax.random.fold_in(splits[5], 71), 0),
        "w_out": gaussian(splits[4], (D, D), D ** -0.5, 0.09375, ((0, 512),)),
    }


score_scale = 0.08838834764831845


def reference(q_text, kv_text, patch_rows, image_count, w_out):
    total_len = q_text.shape[0]
    per = HQ // KVH
    ends = jnp.cumsum(image_count).astype(jnp.int32)
    starts = ends - image_count
    local = jnp.arange(TOK_DEV, dtype=jnp.int32)
    first = TOK_DEV - image_count
    is_image = (local[None, :] >= first[:, None]).reshape(-1)
    index = jnp.clip(starts[:, None] + local[None, :] - first[:, None], 0, IMAGE_ROWS - 1)
    flat = ((index % N_CTX) * IMG_DEV + index // N_CTX).reshape(-1).astype(jnp.int32)
    picked = jnp.take(patch_rows, flat, axis=0).reshape(total_len, KVH, per + 2, HD)
    text = jnp.concatenate([q_text.reshape(total_len, KVH, per, HD), kv_text.reshape(total_len, KVH, 2, HD)], axis=2)
    rows = jnp.where(is_image[:, None, None, None], picked, text)
    queries = rows[:, :, :per]
    keys = rows[:, :, per].astype(jnp.float32)
    values = rows[:, :, per + 1].astype(jnp.float32)
    key_pos = jnp.arange(total_len, dtype=jnp.int32)

    def block(start):
        query = lax.dynamic_slice_in_dim(queries, start, TOK_DEV, 0).astype(jnp.float32)
        scores = jnp.einsum("bgtd,kgd->gtbk", query, keys) * score_scale
        query_pos = start + jnp.arange(TOK_DEV, dtype=jnp.int32)
        allowed = key_pos[None, :] <= query_pos[:, None]
        scores = jnp.where(allowed, scores, jnp.float32(-1e30))
        top = jnp.max(scores, axis=-1, keepdims=True)
        expo = jnp.where(allowed, jnp.exp(scores - top), jnp.float32(0.0))
        total = jnp.sum(expo, axis=-1)
        weights = lax.optimization_barrier(expo.astype(jnp.bfloat16)).astype(jnp.float32)
        numer = jnp.einsum("gtbk,kgd->bgtd", weights, values)
        attended = numer / jnp.transpose(total, (2, 0, 1))[..., None]
        return attended.astype(jnp.bfloat16).reshape(TOK_DEV, D)

    block_starts = jnp.arange(N_CTX, dtype=jnp.int32) * TOK_DEV
    attended = lax.map(block, block_starts).reshape(total_len, D)
    return jnp.dot(attended, w_out, preferred_element_type=jnp.float32).astype(jnp.bfloat16)
```

```python
import functools

import jax
import jax.numpy as jnp
from jax import lax
from jax.experimental import pallas as pl
from jax.experimental.pallas import tpu as pltpu
from jax.sharding import PartitionSpec as P

HD = 128
HEADS = 7
BLK = 128
NZ, NY = 16, 4
BF = jnp.bfloat16
F32 = jnp.float32
NT = (((1,), (1,)), ((), ()))
SCORE_SCALE = 0.08838834764831845 * 1.4426950408889634
MESH = pl.DeviceIdType.MESH


def attention_kernel(
    q_ref, kv_ref, out_ref, buf, top, acc,
    z_send, z_recv, y_send, y_recv, h_send, h_recv, sib_send, sib_recv,
):
    ctx = lax.axis_index("ctx")
    tp = lax.axis_index("tp")
    z, y, xh = ctx // 8, (ctx // 2) % 4, ctx % 2
    xl, core = tp // 2, tp % 2
    y_up, y_down, y_far = (y + 1) % 4, (y + 3) % 4, (y + 2) % 4

    def device(z_, y_, core_):
        return ((z_ * 4 + y_) * 2 + xh, xl * 2 + core_)

    def copy(src, dst, send, recv, z_, y_, core_):
        return pltpu.make_async_remote_copy(
            src_ref=src, dst_ref=dst, send_sem=send, recv_sem=recv,
            device_id=device(z_, y_, core_), device_id_type=MESH,
        )

    def z_copy(way, step, group, kind):
        part = buf.at[0, group, y] if kind == 0 else buf.at[1, group]
        z_to = (z + 17 - 2 * way) % NZ
        return copy(part, part, z_send.at[way, step], z_recv.at[group], z_to, y, core)

    def y_copy(way, group, kind):
        part = buf.at[kind, group, y]
        return copy(part, part, y_send.at[way, group], y_recv.at[way, group],
                    z, (y + 1 + 2 * way) % 4, core)

    def far_copy(group):
        part = buf.at[1, group, y]
        return copy(part, part, h_send.at[0, group], h_recv.at[0, group], z, y_far, core)

    def half_copy(way, group):
        rows = pl.ds(way * 64, 64)
        part = buf.at[0, group, (y + 3 + 2 * way) % 4, rows]
        return copy(part, part, h_send.at[way, group], h_recv.at[way, group],
                    z, (y + 1 + 2 * way) % 4, core)

    def sib_copy(group):
        part = buf.at[core, group]
        return copy(part, part, sib_send.at[group], sib_recv.at[group], z, y, 1 - core)

    def group_at(way, step):
        return (z + NZ - step + 2 * step * way) % NZ

    barrier = pltpu.get_barrier_semaphore()
    for z_, y_, core_ in (
        ((z + 1) % NZ, y, core), ((z + NZ - 1) % NZ, y, core),
        (z, y_up, core), (z, y_down, core), (z, y_far, core), (z, y, 1 - core),
    ):
        pl.semaphore_signal(barrier, inc=1, device_id=device(z_, y_, core_), device_id_type=MESH)
    buf[core, z, y] = kv_ref[...]
    top[...] = jnp.full_like(top, -1e30)
    acc[...] = jnp.zeros_like(acc)
    pl.semaphore_wait(barrier, 6)

    @pl.when(core == 0)
    def _():
        for way in range(2):
            z_copy(way, 0, z, 0).start()
            y_copy(way, z, 0).start()

    @pl.when(core == 1)
    def _():
        y_copy(0, z, 1).start()
        y_copy(1, z, 1).start()
        far_copy(z).start()
        y_copy(0, z, 1).wait_recv()
        y_copy(1, z, 1).wait_recv()
        far_copy(z).wait_recv()
        z_copy(0, 0, z, 1).start()
        z_copy(1, 0, z, 1).start()
        sib_copy(z).start()

    def attend(group, masked):
        keys_values = jnp.concatenate(
            [buf[0, group].reshape(NY * BLK, 2 * HD), buf[1, group].reshape(NY * BLK, 2 * HD)], axis=0
        )
        keys = keys_values[:, :HD]
        values = keys_values[:, HD:]
        values = jnp.concatenate([values, jnp.ones_like(values)], axis=1)
        if masked:
            lane = lax.broadcasted_iota(jnp.int32, (BLK, 2 * NY * BLK), 1)
            place = (((lane // BLK) % NY) * 2 + lane // (NY * BLK)) * BLK + lane % BLK
            row = lax.broadcasted_iota(jnp.int32, (BLK, 2 * NY * BLK), 0)
            allowed = place <= (y * 2 + core) * BLK + row
        for head in range(HEADS):
            rows = pl.ds(head * BLK, BLK)
            scores = lax.dot_general(
                q_ref[:, head * HD:(head + 1) * HD], keys, NT, preferred_element_type=F32
            ) * SCORE_SCALE
            if masked:
                scores = jnp.where(allowed, scores, F32(-1e30))
            old = top[rows, :]
            new = jnp.maximum(old, jnp.max(scores, axis=1, keepdims=True))
            top[rows, :] = new
            shrink = jnp.exp2(old - new)
            weights = jnp.exp2(scores - new[:, :1]).astype(BF)
            added = jnp.dot(weights, values, preferred_element_type=F32)
            acc[rows, :] = acc[rows, :] * jnp.concatenate([shrink, shrink], axis=1) + added

    def turn(t, carry):
        step, way = 1 + t // 2, t % 2
        last = 8 - way

        @pl.when(core == 0)
        def _():
            @pl.when(step <= last)
            def _():
                group = group_at(way, step)
                z_copy(way, step, group, 0).wait_recv()

                @pl.when(step < last)
                def _():
                    z_copy(way, step, group, 0).start()

                y_copy(0, group, 0).start()
                y_copy(1, group, 0).start()

            @pl.when((step - 1 <= last) & ((step > 1) | (way == 0)))
            def _():
                group = group_at(way, step - 1)
                y_copy(0, group, 0).wait_recv()
                y_copy(1, group, 0).wait_recv()
                half_copy(0, group).start()
                half_copy(1, group).start()

            @pl.when((step >= 2) & (step - 2 <= last) & ((step > 2) | (way == 0)))
            def _():
                group = group_at(way, step - 2)
                half_copy(0, group).wait_recv()
                half_copy(1, group).wait_recv()
                sib_copy(group).start()

        @pl.when(core == 1)
        def _():
            @pl.when(step <= last)
            def _():
                group = group_at(way, step)
                z_copy(way, step, group, 1).wait_recv()

                @pl.when(step < last)
                def _():
                    z_copy(way, step, group, 1).start()

                sib_copy(group).start()

        @pl.when((step >= 3) & (step - 3 <= last) & ((step > 3) | (way == 0)))
        def _():
            group = group_at(way, step - 3)
            sib_copy(group).wait_recv()

            @pl.when(group == z)
            def _():
                attend(group, True)

            @pl.when(group < z)
            def _():
                attend(group, False)

        return carry

    lax.fori_loop(0, 22, turn, 0)

    for head in range(HEADS):
        rows = slice(head * BLK, (head + 1) * BLK)
        out_ref[:, head * HD:(head + 1) * HD] = (acc[rows, :HD] / acc[rows, HD:]).astype(BF)

    def settle_group(group, carry):
        sib_copy(group).wait_send()

        @pl.when(core == 0)
        def _():
            for way in range(2):
                y_copy(way, group, 0).wait_send()
                half_copy(way, group).wait_send()

        return carry

    def settle_step(step, carry):
        for kind in range(2):
            @pl.when(core == kind)
            def _():
                z_copy(0, step, z, kind).wait_send()

                @pl.when(step < 7)
                def _():
                    z_copy(1, step, z, kind).wait_send()

        return carry

    lax.fori_loop(0, NZ, settle_group, 0)
    lax.fori_loop(0, 8, settle_step, 0)

    @pl.when(core == 1)
    def _():
        y_copy(0, z, 1).wait_send()
        y_copy(1, z, 1).wait_send()
        far_copy(z).wait_send()


def attention(queries, keys_values):
    vmem = pl.BlockSpec(memory_space=pltpu.VMEM)
    dma = pltpu.SemaphoreType.DMA
    return pl.pallas_call(
        attention_kernel,
        out_shape=jax.ShapeDtypeStruct((BLK, HEADS * HD), BF),
        in_specs=[vmem, vmem],
        out_specs=vmem,
        scratch_shapes=[
            pltpu.VMEM((2, NZ, NY, BLK, 2 * HD), BF),
            pltpu.VMEM((HEADS * BLK, HD), F32),
            pltpu.VMEM((HEADS * BLK, 2 * HD), F32),
            dma((2, 9)), dma((NZ,)),
            dma((2, NZ)), dma((2, NZ)),
            dma((2, NZ)), dma((2, NZ)),
            dma((NZ,)), dma((NZ,)),
        ],
        compiler_params=pltpu.CompilerParams(
            collective_id=0, has_side_effects=True, vmem_limit_bytes=40 * 2**20
        ),
        name="gather_attend",
    )(queries, keys_values)


def swap_core(value):
    pairs = []
    for ctx in range(lax.axis_size("ctx")):
        for tp in range(lax.axis_size("tp")):
            xh, core = ctx % 2, tp % 2
            pairs.append((ctx * 4 + tp, (ctx - xh + core) * 4 + tp - core + xh))
    return lax.ppermute(value, ("ctx", "tp"), pairs)


def body(q_text, kv_text, patch_rows, image_count, w_out):
    tok = q_text.shape[0]
    qcols = q_text.shape[1]
    width = patch_rows.shape[1]
    img_rows = patch_rows.shape[0]
    shards = lax.axis_size("ctx")
    me = lax.axis_index("ctx")
    cap = (tok + shards - 1) // shards
    ends = jnp.cumsum(image_count)
    starts = ends - image_count
    row_ids = jnp.arange(img_rows, dtype=jnp.int32)
    image_index = me + shards * row_ids
    target = jnp.sum((ends[None, :] <= image_index[:, None]).astype(jnp.int32), axis=1)
    below = jnp.sum((target[None, :] < target[:, None]).astype(jnp.int32), axis=1)
    slot_of = target * cap + row_ids - below
    placing = (jnp.arange(shards * cap, dtype=jnp.int32)[:, None] == slot_of[None, :]).astype(BF)
    outgoing = jnp.dot(placing, patch_rows, preferred_element_type=F32).astype(BF)
    incoming = lax.all_to_all(
        outgoing.reshape(shards, cap, width), "ctx", split_axis=0, concat_axis=0, tiled=True
    )
    my_count = jnp.take(image_count, me)
    my_start = jnp.take(starts, me)
    local = jnp.arange(tok, dtype=jnp.int32)
    first = tok - my_count
    is_image = local >= first
    index = jnp.clip(my_start + local - first, 0, shards * img_rows - 1)
    source = index % shards
    lowest = (my_start - source + shards - 1) // shards
    pick = source * cap + jnp.clip(index // shards - lowest, 0, cap - 1)
    picked = jnp.take(incoming.reshape(shards * cap, width), pick, axis=0)
    text = jnp.concatenate([q_text, kv_text], axis=1)
    rows = jnp.where(is_image[:, None], picked, text)
    rows = swap_core(rows)
    attended = attention(rows[:, :qcols], rows[:, qcols:])
    attended = swap_core(attended)
    partial_sums = jnp.dot(
        attended,
        lax.all_gather(w_out, "ctx", axis=0, tiled=True),
        preferred_element_type=F32,
    )
    return lax.psum_scatter(partial_sums.astype(BF), "tp", scatter_dimension=1, tiled=True)


def solution(mesh):
    in_specs = (P("ctx", "tp"), P("ctx", "tp"), P("ctx", "tp"), P(), P(("tp", "ctx"), None))
    out_specs = P("ctx", "tp")
    return jax.shard_map(body, mesh=mesh, in_specs=in_specs, out_specs=out_specs, check_vma=False)
```

```python
import functools

import jax
import jax.numpy as jnp
from jax import lax
from jax.experimental import pallas as pl
from jax.experimental.pallas import tpu as pltpu
from jax.sharding import PartitionSpec as P

HD = 128
HEADS = 7
BLK = 128
NZ, NY = 16, 4
BF = jnp.bfloat16
F32 = jnp.float32
NT = (((1,), (1,)), ((), ()))
SCORE_SCALE = 0.08838834764831845 * 1.4426950408889634
MESH = pl.DeviceIdType.MESH
VMEM = pl.BlockSpec(memory_space=pltpu.VMEM)
DMA = pltpu.SemaphoreType.DMA


class Place:
    def __init__(self):
        ctx = lax.axis_index("ctx")
        tp = lax.axis_index("tp")
        self.z, self.y, self.xh = ctx // 8, (ctx // 2) % 4, ctx % 2
        self.xl, self.core = tp // 2, tp % 2
        self.x = self.xh * 2 + self.xl

    def device(self, z=None, y=None, x=None, core=None):
        z = self.z if z is None else z
        y = self.y if y is None else y
        x = self.x if x is None else x
        core = self.core if core is None else core
        return ((z * 4 + y) * 2 + x // 2, (x % 2) * 2 + core)

    def copy(self, src, dst, send, recv, **where):
        return pltpu.make_async_remote_copy(
            src_ref=src, dst_ref=dst, send_sem=send, recv_sem=recv,
            device_id=self.device(**where), device_id_type=MESH,
        )

    def greet(self, wheres):
        barrier = pltpu.get_barrier_semaphore()
        for where in wheres:
            pl.semaphore_signal(
                barrier, inc=1, device_id=self.device(**where), device_id_type=MESH
            )
        return barrier

    def ring_neighbours(self):
        z, y = self.z, self.y
        return [
            dict(z=(z + 1) % NZ), dict(z=(z + NZ - 1) % NZ),
            dict(y=(y + 1) % NY), dict(y=(y + 3) % NY), dict(y=(y + 2) % NY),
            dict(core=1 - self.core),
        ]


SPREAD_SEMS = [
    DMA((2, 9)), DMA((NZ,)), DMA((2, NZ)), DMA((2, NZ)), DMA((2, NZ)), DMA((2, NZ)),
    DMA((NZ,)), DMA((NZ,)),
]


class Spread:
    def __init__(self, place, buf, sems, half):
        self.p, self.buf, self.half = place, buf, half
        (self.z_send, self.z_recv, self.y_send, self.y_recv,
         self.h_send, self.h_recv, self.sib_send, self.sib_recv) = sems

    def z_copy(self, way, step, group, kind):
        p = self.p
        part = self.buf.at[0, group, p.y] if kind == 0 else self.buf.at[1, group]
        return p.copy(part, part, self.z_send.at[way, step], self.z_recv.at[group],
                      z=(p.z + 17 - 2 * way) % NZ)

    def y_copy(self, way, group, kind):
        p = self.p
        part = self.buf.at[kind, group, p.y]
        return p.copy(part, part, self.y_send.at[way, group], self.y_recv.at[way, group],
                      y=(p.y + 1 + 2 * way) % NY)

    def far_copy(self, group):
        p = self.p
        part = self.buf.at[1, group, p.y]
        return p.copy(part, part, self.h_send.at[0, group], self.h_recv.at[0, group],
                      y=(p.y + 2) % NY)

    def half_copy(self, way, group):
        p = self.p
        part = self.half(self.buf.at[0, group, (p.y + 3 + 2 * way) % NY], way)
        return p.copy(part, part, self.h_send.at[way, group], self.h_recv.at[way, group],
                      y=(p.y + 1 + 2 * way) % NY)

    def sib_copy(self, group):
        p = self.p
        part = self.buf.at[p.core, group]
        return p.copy(part, part, self.sib_send.at[group], self.sib_recv.at[group],
                      core=1 - p.core)

    def group_at(self, way, step):
        return (self.p.z + NZ - step + 2 * step * way) % NZ

    def begin(self):
        p = self.p

        @pl.when(p.core == 0)
        def _():
            for way in range(2):
                self.z_copy(way, 0, p.z, 0).start()
                self.y_copy(way, p.z, 0).start()

        @pl.when(p.core == 1)
        def _():
            first = [self.y_copy(0, p.z, 1), self.y_copy(1, p.z, 1), self.far_copy(p.z)]
            for copy in first:
                copy.start()
            for copy in first:
                copy.wait_recv()
            self.z_copy(0, 0, p.z, 1).start()
            self.z_copy(1, 0, p.z, 1).start()
            self.sib_copy(p.z).start()

    def advance(self, step, way):
        p = self.p
        last = 8 - way

        @pl.when(p.core == 0)
        def _():
            @pl.when(step <= last)
            def _():
                group = self.group_at(way, step)
                self.z_copy(way, step, group, 0).wait_recv()

                @pl.when(step < last)
                def _():
                    self.z_copy(way, step, group, 0).start()

                self.y_copy(0, group, 0).start()
                self.y_copy(1, group, 0).start()

            @pl.when((step - 1 <= last) & ((step > 1) | (way == 0)))
            def _():
                group = self.group_at(way, step - 1)
                self.y_copy(0, group, 0).wait_recv()
                self.y_copy(1, group, 0).wait_recv()
                self.half_copy(0, group).start()
                self.half_copy(1, group).start()

            @pl.when((step >= 2) & (step - 2 <= last) & ((step > 2) | (way == 0)))
            def _():
                group = self.group_at(way, step - 2)
                self.half_copy(0, group).wait_recv()
                self.half_copy(1, group).wait_recv()
                self.sib_copy(group).start()

        @pl.when(p.core == 1)
        def _():
            @pl.when(step <= last)
            def _():
                group = self.group_at(way, step)
                self.z_copy(way, step, group, 1).wait_recv()

                @pl.when(step < last)
                def _():
                    self.z_copy(way, step, group, 1).start()

                self.sib_copy(group).start()

    def arrived(self, step, way, then):
        @pl.when((step >= 3) & (step - 3 <= 8 - way) & ((step > 3) | (way == 0)))
        def _():
            group = self.group_at(way, step - 3)
            self.sib_copy(group).wait_recv()
            if then is not None:
                then(group)

    def settle(self):
        p = self.p

        def settle_group(group, carry):
            self.sib_copy(group).wait_send()

            @pl.when(p.core == 0)
            def _():
                for way in range(2):
                    self.y_copy(way, group, 0).wait_send()
                    self.half_copy(way, group).wait_send()

            return carry

        def settle_step(step, carry):
            for kind in range(2):
                @pl.when(p.core == kind)
                def _():
                    self.z_copy(0, step, p.z, kind).wait_send()

                    @pl.when(step < 7)
                    def _():
                        self.z_copy(1, step, p.z, kind).wait_send()

            return carry

        lax.fori_loop(0, NZ, settle_group, 0)
        lax.fori_loop(0, 8, settle_step, 0)

        @pl.when(p.core == 1)
        def _():
            self.y_copy(0, p.z, 1).wait_send()
            self.y_copy(1, p.z, 1).wait_send()
            self.far_copy(p.z).wait_send()


def attention_kernel(q_ref, kv_ref, out_ref, buf, top, acc, *sems):
    p = Place()
    spread = Spread(p, buf, sems, lambda block, way: block.at[pl.ds(way * 64, 64)])
    barrier = p.greet(p.ring_neighbours())
    buf[p.core, p.z, p.y] = kv_ref[...]
    top[...] = jnp.full_like(top, -1e30)
    acc[...] = jnp.zeros_like(acc)
    pl.semaphore_wait(barrier, 6)
    spread.begin()

    def attend(group, masked):
        keys_values = jnp.concatenate(
            [buf[0, group].reshape(NY * BLK, 2 * HD), buf[1, group].reshape(NY * BLK, 2 * HD)], axis=0
        )
        keys = keys_values[:, :HD]
        values = keys_values[:, HD:]
        values = jnp.concatenate([values, jnp.ones_like(values)], axis=1)
        if masked:
            lane = lax.broadcasted_iota(jnp.int32, (BLK, 2 * NY * BLK), 1)
            position = (((lane // BLK) % NY) * 2 + lane // (NY * BLK)) * BLK + lane % BLK
            row = lax.broadcasted_iota(jnp.int32, (BLK, 2 * NY * BLK), 0)
            allowed = position <= (p.y * 2 + p.core) * BLK + row
        for head in range(HEADS):
            rows = pl.ds(head * BLK, BLK)
            scores = lax.dot_general(
                q_ref[:, head * HD:(head + 1) * HD], keys, NT, preferred_element_type=F32
            ) * SCORE_SCALE
            if masked:
                scores = jnp.where(allowed, scores, F32(-1e30))
            old = top[rows, :]
            new = jnp.maximum(old, jnp.max(scores, axis=1, keepdims=True))
            top[rows, :] = new
            shrink = jnp.exp2(old - new)
            weights = jnp.exp2(scores - new[:, :1]).astype(BF)
            added = jnp.dot(weights, values, preferred_element_type=F32)
            acc[rows, :] = acc[rows, :] * jnp.concatenate([shrink, shrink], axis=1) + added

    def attend_any(group):
        @pl.when(group == p.z)
        def _():
            attend(group, True)

        @pl.when(group < p.z)
        def _():
            attend(group, False)

    def turn(t, carry):
        step, way = 1 + t // 2, t % 2
        spread.advance(step, way)
        spread.arrived(step, way, attend_any)
        return carry

    lax.fori_loop(0, 22, turn, 0)
    for head in range(HEADS):
        rows = slice(head * BLK, (head + 1) * BLK)
        out_ref[:, head * HD:(head + 1) * HD] = (acc[rows, :HD] / acc[rows, HD:]).astype(BF)
    spread.settle()


def attention(queries, keys_values):
    return pl.pallas_call(
        attention_kernel,
        out_shape=jax.ShapeDtypeStruct((BLK, HEADS * HD), BF),
        in_specs=[VMEM, VMEM],
        out_specs=VMEM,
        scratch_shapes=[
            pltpu.VMEM((2, NZ, NY, BLK, 2 * HD), BF),
            pltpu.VMEM((HEADS * BLK, HD), F32),
            pltpu.VMEM((HEADS * BLK, 2 * HD), F32),
            *SPREAD_SEMS,
        ],
        compiler_params=pltpu.CompilerParams(
            collective_id=0, has_side_effects=True, vmem_limit_bytes=40 * 2**20
        ),
        name="gather_attend",
    )(queries, keys_values)


QCOLS = HEADS * HD
PIECE = 16


def weight_kernel(piece_ref, w_ref, pieces, x_send, x_recv, own_sem, merged, *sems):
    p = Place()
    spread = Spread(p, w_ref, sems, lambda block, way: block.at[way])
    barrier = p.greet(p.ring_neighbours() + [dict(x=(p.x + j) % 4) for j in (1, 2, 3)])
    pl.semaphore_wait(barrier, 9)

    def columns(x):
        return (x % 2) * 2 + x // 2

    def x_copy(j):
        x = (p.x + j) % 4
        return p.copy(piece_ref.at[columns(x)], pieces.at[p.x], x_send.at[j - 1], x_recv.at[j - 1],
                      x=x)

    def x_arrival(j):
        x = (p.x + 4 - j) % 4
        return p.copy(pieces.at[x], pieces.at[x], x_send.at[j - 1], x_recv.at[j - 1], x=x)

    for j in (1, 2, 3):
        x_copy(j).start()
    pieces[p.x] = piece_ref[columns(p.x)]
    for j in (1, 2, 3):
        x_arrival(j).wait_recv()
    for xl in range(2):
        merged[xl] = pieces[xl] + pieces[2 + xl]
    own = pltpu.make_async_copy(merged, w_ref.at[p.core, p.z, p.y], own_sem)
    own.start()
    own.wait()
    spread.begin()

    def turn(t, carry):
        step, way = 1 + t // 2, t % 2
        spread.advance(step, way)
        spread.arrived(step, way, None)
        return carry

    lax.fori_loop(0, 22, turn, 0)
    for j in (1, 2, 3):
        x_copy(j).wait_send()
    spread.settle()


def gather_weights(w_out):
    xh = lax.axis_index("ctx") % 2
    rows = w_out.shape[0]
    piece = jnp.where(
        xh == 0,
        jnp.pad(w_out, ((0, PIECE - rows), (0, 0))),
        jnp.pad(w_out, ((rows, PIECE - 2 * rows), (0, 0))),
    )
    piece = jnp.transpose(piece.reshape(PIECE, 4, QCOLS), (1, 0, 2))
    return pl.pallas_call(
        weight_kernel,
        out_shape=jax.ShapeDtypeStruct((2, NZ, NY, 2, PIECE, QCOLS), BF),
        in_specs=[VMEM],
        out_specs=pl.BlockSpec(memory_space=pl.ANY),
        scratch_shapes=[
            pltpu.VMEM((4, PIECE, QCOLS), BF), DMA((3,)), DMA((3,)), DMA,
            pltpu.VMEM((2, PIECE, QCOLS), BF),
            *SPREAD_SEMS,
        ],
        compiler_params=pltpu.CompilerParams(
            collective_id=1, has_side_effects=True, vmem_limit_bytes=16 * 2**20
        ),
        name="gather_weights",
    )(piece)


def project_kernel(
    att_ref, w_ref, out_ref, w, heads,
    w_sem, x_send, x_recv, h_send, h_recv,
):
    p = Place()
    x_up, x_down, x_far = (p.x + 1) % 4, (p.x + 3) % 4, (p.x + 2) % 4
    depth = NZ * NY * PIECE
    half = BLK // 2
    barrier = p.greet([dict(x=x_up), dict(x=x_down)])
    fetch = pltpu.make_async_copy(w_ref, w, w_sem)
    fetch.start()
    row = lax.broadcasted_iota(jnp.int32, (QCOLS, depth), 0)
    lane = lax.broadcasted_iota(jnp.int32, (QCOLS, depth), 1)
    spot = (lane // PIECE) * (PIECE - 2) + lane % PIECE
    widen = ((row == spot) & (lane % PIECE < PIECE - 2)).astype(F32).astype(BF)
    heads[p.x] = jnp.dot(att_ref[...], widen, preferred_element_type=F32).astype(BF)
    pl.semaphore_wait(barrier, 2)


    def block_copy(way):
        part = heads.at[p.x]
        return p.copy(part, part, x_send.at[way], x_recv.at[way], x=(p.x + 1 + 2 * way) % 4)

    def half_copy(way):
        part = heads.at[(p.x + 3 + 2 * way) % 4, pl.ds(way * half, half)]
        return p.copy(part, part, h_send.at[way], h_recv.at[way], x=(p.x + 1 + 2 * way) % 4)

    def product(x):
        group_xh, group_xl = x // 2, x % 2
        rows = w[group_xh, :, :, group_xl].reshape(depth, QCOLS)
        return jnp.dot(heads[x], rows, preferred_element_type=F32)

    block_copy(0).start()
    block_copy(1).start()
    fetch.wait()
    total = product(p.x)
    block_copy(0).wait_recv()
    half_copy(0).start()
    block_copy(1).wait_recv()
    half_copy(1).start()
    total += product(x_down)
    total += product(x_up)
    half_copy(0).wait_recv()
    half_copy(1).wait_recv()
    total += product(x_far)
    out_ref[...] = total.astype(BF)
    for way in range(2):
        block_copy(way).wait_send()
        half_copy(way).wait_send()


def project(attended, weights):
    return pl.pallas_call(
        project_kernel,
        out_shape=jax.ShapeDtypeStruct((BLK, QCOLS), BF),
        in_specs=[VMEM, pl.BlockSpec(memory_space=pl.ANY)],
        out_specs=VMEM,
        scratch_shapes=[
            pltpu.VMEM((2, NZ, NY, 2, PIECE, QCOLS), BF),
            pltpu.VMEM((4, BLK, NZ * NY * PIECE), BF),

            DMA, DMA((2,)), DMA((2,)), DMA((2,)), DMA((2,)),
        ],
        compiler_params=pltpu.CompilerParams(
            collective_id=2, has_side_effects=True, vmem_limit_bytes=48 * 2**20
        ),
        name="project",
    )(attended, weights)


def swap_core(value):
    pairs = []
    for ctx in range(lax.axis_size("ctx")):
        for tp in range(lax.axis_size("tp")):
            xh, core = ctx % 2, tp % 2
            pairs.append((ctx * 4 + tp, (ctx - xh + core) * 4 + tp - core + xh))
    return lax.ppermute(value, ("ctx", "tp"), pairs)


def body(q_text, kv_text, patch_rows, image_count, w_out):
    weights = gather_weights(w_out)
    tok = q_text.shape[0]
    qcols = q_text.shape[1]
    width = patch_rows.shape[1]
    img_rows = patch_rows.shape[0]
    shards = lax.axis_size("ctx")
    me = lax.axis_index("ctx")
    cap = (tok + shards - 1) // shards
    ends = jnp.cumsum(image_count)
    starts = ends - image_count
    row_ids = jnp.arange(img_rows, dtype=jnp.int32)
    image_index = me + shards * row_ids
    target = jnp.sum((ends[None, :] <= image_index[:, None]).astype(jnp.int32), axis=1)
    below = jnp.sum((target[None, :] < target[:, None]).astype(jnp.int32), axis=1)
    slot_of = target * cap + row_ids - below
    placing = (jnp.arange(shards * cap, dtype=jnp.int32)[:, None] == slot_of[None, :]).astype(BF)
    outgoing = jnp.dot(placing, patch_rows, preferred_element_type=F32).astype(BF)
    incoming = lax.all_to_all(
        outgoing.reshape(shards, cap, width), "ctx", split_axis=0, concat_axis=0, tiled=True
    )
    my_count = jnp.take(image_count, me)
    my_start = jnp.take(starts, me)
    local = jnp.arange(tok, dtype=jnp.int32)
    first = tok - my_count
    is_image = local >= first
    index = jnp.clip(my_start + local - first, 0, shards * img_rows - 1)
    source = index % shards
    lowest = (my_start - source + shards - 1) // shards
    pick = source * cap + jnp.clip(index // shards - lowest, 0, cap - 1)
    picked = jnp.take(incoming.reshape(shards * cap, width), pick, axis=0)
    text = jnp.concatenate([q_text, kv_text], axis=1)
    rows = jnp.where(is_image[:, None], picked, text)
    rows = swap_core(rows)
    attended = attention(rows[:, :qcols], rows[:, qcols:])
    return swap_core(project(attended, weights))


def solution(mesh):
    in_specs = (P("ctx", "tp"), P("ctx", "tp"), P("ctx", "tp"), P(), P(("tp", "ctx"), None))
    out_specs = P("ctx", "tp")
    return jax.shard_map(body, mesh=mesh, in_specs=in_specs, out_specs=out_specs, check_vma=False)
```

```python
import functools

import jax
import jax.numpy as jnp
from jax import lax
from jax.experimental import pallas as pl
from jax.experimental.pallas import tpu as pltpu
from jax.sharding import PartitionSpec as P

HD = 128
HEADS = 7
BLK = 128
NZ, NY = 16, 4
BF = jnp.bfloat16
F32 = jnp.float32
NT = (((1,), (1,)), ((), ()))
SCORE_SCALE = 0.08838834764831845 * 1.4426950408889634
MESH = pl.DeviceIdType.MESH
VMEM = pl.BlockSpec(memory_space=pltpu.VMEM)
DMA = pltpu.SemaphoreType.DMA


class Place:
    def __init__(self):
        ctx = lax.axis_index("ctx")
        tp = lax.axis_index("tp")
        self.z, self.y, self.xh = ctx // 8, (ctx // 2) % 4, ctx % 2
        self.xl, self.core = tp // 2, tp % 2
        self.x = self.xh * 2 + self.xl

    def device(self, z=None, y=None, x=None, core=None):
        z = self.z if z is None else z
        y = self.y if y is None else y
        x = self.x if x is None else x
        core = self.core if core is None else core
        return ((z * 4 + y) * 2 + x // 2, (x % 2) * 2 + core)

    def copy(self, src, dst, send, recv, **where):
        return pltpu.make_async_remote_copy(
            src_ref=src, dst_ref=dst, send_sem=send, recv_sem=recv,
            device_id=self.device(**where), device_id_type=MESH,
        )

    def greet(self, wheres):
        barrier = pltpu.get_barrier_semaphore()
        for where in wheres:
            pl.semaphore_signal(
                barrier, inc=1, device_id=self.device(**where), device_id_type=MESH
            )
        return barrier

    def ring_neighbours(self):
        z, y = self.z, self.y
        return [
            dict(z=(z + 1) % NZ), dict(z=(z + NZ - 1) % NZ),
            dict(y=(y + 1) % NY), dict(y=(y + 3) % NY), dict(y=(y + 2) % NY),
            dict(core=1 - self.core),
        ]


QCOLS = HEADS * HD
PIECE = 16
STEPS = 9
TURNS = 12
SPREAD_SEMS = [
    DMA((2,)), DMA((2,)), DMA((3,)), DMA((3,)), DMA((3,)), DMA((3,)),
    DMA((2, STEPS)), DMA((2, STEPS)), DMA((2, STEPS)), DMA((2, STEPS)),
    DMA((2, STEPS)), DMA((2, STEPS)), DMA((2, STEPS)), DMA((2, STEPS)),
]


class Spread:
    def __init__(self, place, one, row, half, sems):
        self.p, self.one, self.row, self.half = place, one, row, half
        (self.w_send, self.w_recv, self.f_send, self.f_recv, self.o_send, self.o_recv,
         self.z_send, self.z_recv,
         self.y_send, self.y_recv, self.h_send, self.h_recv, self.s_send, self.s_recv) = sems
        self.last = 8 - place.core

    def group(self, way, step):
        return (self.p.z + NZ - step + 2 * step * way) % NZ

    def waits(self, ref, sem):
        self.p.copy(ref, ref, self.w_send.at[0], sem, core=1 - self.p.core).wait_recv()

    def z_part(self, part, step):
        p, group = self.p, self.group(self.p.core, step)
        return self.one(0, group, p.y) if part == 0 else self.row(1, group)

    def z_copy(self, part, step):
        p, ref = self.p, self.z_part(part, step)
        return p.copy(ref, ref, self.z_send.at[part, step], self.z_recv.at[part, step + 1],
                      z=(p.z + 17 - 2 * p.core) % NZ)

    def y_copy(self, way, step):
        p = self.p
        ref = self.one(0, self.group(p.core, step), p.y)
        return p.copy(ref, ref, self.y_send.at[way, step], self.y_recv.at[way, step],
                      y=(p.y + 1 + 2 * way) % NY)

    def half_copy(self, way, step):
        p = self.p
        ref = self.half(self.one(0, self.group(p.core, step), (p.y + 3 + 2 * way) % NY), way)
        return p.copy(ref, ref, self.h_send.at[way, step], self.h_recv.at[way, step],
                      y=(p.y + 1 + 2 * way) % NY)

    def first_copy(self, j):
        p, ref = self.p, self.one(1, self.p.z, self.p.y)
        return p.copy(ref, ref, self.f_send.at[j], self.f_recv.at[j], y=(p.y + 1 + j) % NY)

    def sib_copy(self, part, step):
        p = self.p
        ref = self.row(part, self.group(p.core, step))
        return p.copy(ref, ref, self.s_send.at[part, step], self.s_recv.at[part, step],
                      core=1 - p.core)

    def own_copy(self, j):
        p = self.p
        ref = self.one(0, p.z, (p.y + 1 + j) % NY)
        return p.copy(ref, ref, self.o_send.at[j], self.o_recv.at[j], core=1 - p.core)

    def begin(self):
        self.z_copy(0, 0).start()
        for j in range(3):
            self.first_copy(j).start()

        @pl.when(self.p.core == 0)
        def _():
            self.y_copy(0, 0).start()
            self.y_copy(1, 0).start()

    def begin_b(self):
        for j in range(3):
            self.first_copy(j).wait_recv()
        self.z_copy(1, 0).start()

    def along_z(self, step):
        for part in range(2):
            @pl.when(step <= self.last)
            def _():
                self.waits(self.z_part(part, step), self.z_recv.at[part, step])

                @pl.when(step < self.last)
                def _():
                    self.z_copy(part, step).start()

                if part == 0:
                    self.y_copy(0, step).start()
                    self.y_copy(1, step).start()
                else:
                    self.sib_copy(1, step).start()

    def along_y(self, step):
        core = self.p.core

        @pl.when((step - 1 <= self.last) & (step - 1 >= core))
        def _():
            for way in range(2):
                self.y_copy(way, step - 1).wait_recv()
                self.half_copy(way, step - 1).start()

        @pl.when((step - 2 <= self.last) & (step - 2 >= core))
        def _():
            for way in range(2):
                self.half_copy(way, step - 2).wait_recv()

            @pl.when(step > 2)
            def _():
                self.sib_copy(0, step - 2).start()

            @pl.when(step == 2)
            def _():
                for j in range(3):
                    self.own_copy(j).start()

    def own_arrived(self):
        @pl.when(self.p.core == 1)
        def _():
            for j in range(3):
                self.own_copy(j).wait_recv()

    def sib_arrived(self, step):
        group = self.group(1 - self.p.core, step)
        for part in range(2):
            self.waits(self.row(part, group), self.s_recv.at[part, step])

    def settle(self):
        core = self.p.core
        for j in range(3):
            self.first_copy(j).wait_send()

        @pl.when(core == 0)
        def _():
            for j in range(3):
                self.own_copy(j).wait_send()

        def settle_step(step, carry):
            for part in range(2):
                @pl.when(step < self.last)
                def _():
                    self.z_copy(part, step).wait_send()

                @pl.when((step <= self.last) & (step > 0))
                def _():
                    self.sib_copy(part, step).wait_send()

            @pl.when((step <= self.last) & (step >= core))
            def _():
                for way in range(2):
                    self.y_copy(way, step).wait_send()
                    self.half_copy(way, step).wait_send()

            return carry

        lax.fori_loop(0, STEPS, settle_step, 0)


def columns_of(x):
    return (x % 2) * 2 + x // 2


def layer_kernel(
    q_ref, kv_ref, piece_ref, out_ref, buf, w, pieces, heads, top, acc,
    wx_send, wx_recv, ax_send, ax_recv, ah_send, ah_recv, *sems,
):
    p = Place()
    keys_values = Spread(
        p, lambda part, z, y: buf.at[part, z, y], lambda part, z: buf.at[part, z],
        lambda block, way: block.at[pl.ds(way * 64, 64)], sems[:14],
    )
    groups = (pl.ds(0, 3), pl.ds(3, 1))
    halves = (pl.ds(0, 2), pl.ds(2, 1))
    weights = Spread(
        p, lambda part, z, y: w.at[z, y, groups[part]], lambda part, z: w.at[z, :, groups[part]],
        lambda block, way: block.at[halves[way]], sems[14:],
    )
    barrier = p.greet(p.ring_neighbours() + [dict(x=(p.x + j) % 4) for j in (1, 2, 3)])
    top[...] = jnp.full_like(top, -1e30)
    acc[...] = jnp.zeros_like(acc)
    buf[p.core, p.z, p.y] = kv_ref[...]
    pieces[p.x] = piece_ref[columns_of(p.x)]
    pl.semaphore_wait(barrier, 9)

    def kv_swap():
        ref = buf.at[p.core, p.z, p.y]
        return p.copy(ref, ref, keys_values.w_send.at[0], keys_values.w_recv.at[0], core=1 - p.core)

    def w_swap(xl):
        ref = w.at[p.z, p.y, 2 * xl + p.core]
        return p.copy(ref, ref, weights.w_send.at[xl], weights.w_recv.at[xl], core=1 - p.core)

    def piece_copy(j):
        x = (p.x + j) % 4
        return p.copy(piece_ref.at[columns_of(x)], pieces.at[p.x], wx_send.at[j - 1],
                      wx_recv.at[j - 1], x=x)

    def piece_from(j):
        x = (p.x + 4 - j) % 4
        return p.copy(pieces.at[x], pieces.at[x], wx_send.at[j - 1], wx_recv.at[j - 1], x=x)

    kv_swap().start()
    for j in (1, 2, 3):
        piece_copy(j).start()
    keys_values.waits(buf.at[1 - p.core, p.z, p.y], keys_values.w_recv.at[0])
    keys_values.begin()
    for j in (1, 2, 3):
        piece_from(j).wait_recv()
    for xl in range(2):
        w[p.z, p.y, 2 * xl + p.core] = pieces[xl] + pieces[2 + xl]
        w_swap(xl).start()
    keys_values.begin_b()
    for xl in range(2):
        weights.waits(w.at[p.z, p.y, 2 * xl + 1 - p.core], weights.w_recv.at[xl])
    weights.begin()

    def attend(group, masked):
        block = jnp.concatenate(
            [buf[0, group].reshape(NY * BLK, 2 * HD), buf[1, group].reshape(NY * BLK, 2 * HD)], axis=0
        )
        keys = block[:, :HD]
        values = block[:, HD:]
        values = jnp.concatenate([values, jnp.ones_like(values)], axis=1)
        if masked:
            lane = lax.broadcasted_iota(jnp.int32, (BLK, 2 * NY * BLK), 1)
            position = (((lane // BLK) % NY) * 2 + lane // (NY * BLK)) * BLK + lane % BLK
            row = lax.broadcasted_iota(jnp.int32, (BLK, 2 * NY * BLK), 0)
            allowed = position <= (p.y * 2 + p.core) * BLK + row
        for head in range(HEADS):
            rows = pl.ds(head * BLK, BLK)
            scores = lax.dot_general(
                q_ref[:, head * HD:(head + 1) * HD], keys, NT, preferred_element_type=F32
            ) * SCORE_SCALE
            if masked:
                scores = jnp.where(allowed, scores, F32(-1e30))
            old = top[rows, :]
            new = jnp.maximum(old, jnp.max(scores, axis=1, keepdims=True))
            top[rows, :] = new
            shrink = jnp.exp2(old - new)
            expo = jnp.exp2(scores - new[:, :1]).astype(BF)
            added = jnp.dot(expo, values, preferred_element_type=F32)
            acc[rows, :] = acc[rows, :] * jnp.concatenate([shrink, shrink], axis=1) + added

    def turn(step, carry):
        keys_values.along_z(step)
        keys_values.along_y(step)

        @pl.when(step == 1)
        def _():
            weights.begin_b()

        weights.along_z(step)
        weights.along_y(step)

        @pl.when(step == 3)
        def _():
            keys_values.own_arrived()
            attend(p.z, True)
            weights.own_arrived()

        def part(j, carry):
            way = (p.core + j) % 2
            back = step - 2 - j
            here = (back >= 1) & (back <= 8 - way)
            group = keys_values.group(way, back)

            @pl.when(here & (j == 1))
            def _():
                keys_values.sib_arrived(back)
                weights.sib_arrived(back)

            @pl.when(here & (group < p.z))
            def _():
                attend(group, False)

            return carry

        lax.fori_loop(0, 2, part, 0)
        return carry

    lax.fori_loop(1, TURNS, turn, 0)

    depth = NZ * NY * PIECE
    row = lax.broadcasted_iota(jnp.int32, (QCOLS, depth), 0)
    lane = lax.broadcasted_iota(jnp.int32, (QCOLS, depth), 1)
    spot = (lane // PIECE) * (PIECE - 2) + lane % PIECE
    widen = ((row == spot) & (lane % PIECE < PIECE - 2)).astype(F32).astype(BF)
    attended = jnp.concatenate(
        [(acc[pl.ds(head * BLK, BLK), :HD] / acc[pl.ds(head * BLK, BLK), HD:]).astype(BF)
         for head in range(HEADS)], axis=1
    )
    heads[p.x] = jnp.dot(attended, widen, preferred_element_type=F32).astype(BF)

    def heads_copy(way):
        ref = heads.at[p.x]
        return p.copy(ref, ref, ax_send.at[way], ax_recv.at[way], x=(p.x + 1 + 2 * way) % 4)

    def heads_half(way):
        ref = heads.at[(p.x + 3 + 2 * way) % 4, pl.ds(way * 64, 64)]
        return p.copy(ref, ref, ah_send.at[way], ah_recv.at[way], x=(p.x + 1 + 2 * way) % 4)

    def product(x):
        rows = w[:, :, columns_of(x)].reshape(depth, QCOLS)
        return jnp.dot(heads[x], rows, preferred_element_type=F32)

    heads_copy(0).start()
    heads_copy(1).start()
    total = product(p.x)
    for way in range(2):
        heads_copy(way).wait_recv()
        heads_half(way).start()
    total += product((p.x + 3) % 4)
    total += product((p.x + 1) % 4)
    for way in range(2):
        heads_half(way).wait_recv()
    total += product((p.x + 2) % 4)
    out_ref[...] = total.astype(BF)

    kv_swap().wait_send()
    for xl in range(2):
        w_swap(xl).wait_send()
    for j in (1, 2, 3):
        piece_copy(j).wait_send()
    for way in range(2):
        heads_copy(way).wait_send()
        heads_half(way).wait_send()
    keys_values.settle()
    weights.settle()


def layer(queries, keys_values, w_out):
    xh = lax.axis_index("ctx") % 2
    rows = w_out.shape[0]
    piece = jnp.where(
        xh == 0,
        jnp.pad(w_out, ((0, PIECE - rows), (0, 0))),
        jnp.pad(w_out, ((rows, PIECE - 2 * rows), (0, 0))),
    )
    piece = jnp.transpose(piece.reshape(PIECE, 4, QCOLS), (1, 0, 2))
    return pl.pallas_call(
        layer_kernel,
        out_shape=jax.ShapeDtypeStruct((BLK, QCOLS), BF),
        in_specs=[VMEM, VMEM, VMEM],
        out_specs=VMEM,
        scratch_shapes=[
            pltpu.VMEM((2, NZ, NY, BLK, 2 * HD), BF),
            pltpu.VMEM((NZ, NY, 4, PIECE, QCOLS), BF),
            pltpu.VMEM((4, PIECE, QCOLS), BF),
            pltpu.VMEM((4, BLK, NZ * NY * PIECE), BF),
            pltpu.VMEM((HEADS * BLK, HD), F32),
            pltpu.VMEM((HEADS * BLK, 2 * HD), F32),
            DMA((3,)), DMA((3,)), DMA((2,)), DMA((2,)), DMA((2,)), DMA((2,)),
            *SPREAD_SEMS, *SPREAD_SEMS,
        ],
        compiler_params=pltpu.CompilerParams(
            collective_id=0, has_side_effects=True, vmem_limit_bytes=50 * 2**20
        ),
        name="layer",
    )(queries, keys_values, piece)


def swap_core(value):
    pairs = []
    for ctx in range(lax.axis_size("ctx")):
        for tp in range(lax.axis_size("tp")):
            xh, core = ctx % 2, tp % 2
            pairs.append((ctx * 4 + tp, (ctx - xh + core) * 4 + tp - core + xh))
    return lax.ppermute(value, ("ctx", "tp"), pairs)


def body(q_text, kv_text, patch_rows, image_count, w_out):
    tok = q_text.shape[0]
    qcols = q_text.shape[1]
    width = patch_rows.shape[1]
    img_rows = patch_rows.shape[0]
    shards = lax.axis_size("ctx")
    me = lax.axis_index("ctx")
    cap = (tok + shards - 1) // shards
    ends = jnp.cumsum(image_count)
    starts = ends - image_count
    row_ids = jnp.arange(img_rows, dtype=jnp.int32)
    image_index = me + shards * row_ids
    target = jnp.sum((ends[None, :] <= image_index[:, None]).astype(jnp.int32), axis=1)
    below = jnp.sum((target[None, :] < target[:, None]).astype(jnp.int32), axis=1)
    slot_of = target * cap + row_ids - below
    placing = (jnp.arange(shards * cap, dtype=jnp.int32)[:, None] == slot_of[None, :]).astype(BF)
    outgoing = jnp.dot(placing, patch_rows, preferred_element_type=F32).astype(BF)
    incoming = lax.all_to_all(
        outgoing.reshape(shards, cap, width), "ctx", split_axis=0, concat_axis=0, tiled=True
    )
    my_count = jnp.take(image_count, me)
    my_start = jnp.take(starts, me)
    local = jnp.arange(tok, dtype=jnp.int32)
    first = tok - my_count
    is_image = local >= first
    index = jnp.clip(my_start + local - first, 0, shards * img_rows - 1)
    source = index % shards
    lowest = (my_start - source + shards - 1) // shards
    pick = source * cap + jnp.clip(index // shards - lowest, 0, cap - 1)
    picked = jnp.take(incoming.reshape(shards * cap, width), pick, axis=0)
    text = jnp.concatenate([q_text, kv_text], axis=1)
    rows = jnp.where(is_image[:, None], picked, text)
    rows = swap_core(rows)
    return swap_core(layer(rows[:, :qcols], rows[:, qcols:], w_out))


def solution(mesh):
    in_specs = (P("ctx", "tp"), P("ctx", "tp"), P("ctx", "tp"), P(), P(("tp", "ctx"), None))
    out_specs = P("ctx", "tp")
    return jax.shard_map(body, mesh=mesh, in_specs=in_specs, out_specs=out_specs, check_vma=False)
```

```python
import functools

import jax
import jax.numpy as jnp
from jax import lax
from jax.experimental import pallas as pl
from jax.experimental.pallas import tpu as pltpu
from jax.sharding import PartitionSpec as P

HD = 128
HEADS = 7
BLK = 128
NZ, NY = 16, 4
BF = jnp.bfloat16
F32 = jnp.float32
NT = (((1,), (1,)), ((), ()))
SCORE_SCALE = 0.08838834764831845 * 1.4426950408889634
MESH = pl.DeviceIdType.MESH
VMEM = pl.BlockSpec(memory_space=pltpu.VMEM)
DMA = pltpu.SemaphoreType.DMA


class Place:
    def __init__(self):
        ctx = lax.axis_index("ctx")
        tp = lax.axis_index("tp")
        self.z, self.y, self.xh = ctx // 8, (ctx // 2) % 4, ctx % 2
        self.xl, self.core = tp // 2, tp % 2
        self.x = self.xh * 2 + self.xl

    def device(self, z=None, y=None, x=None, core=None):
        z = self.z if z is None else z
        y = self.y if y is None else y
        x = self.x if x is None else x
        core = self.core if core is None else core
        return ((z * 4 + y) * 2 + x // 2, (x % 2) * 2 + core)

    def copy(self, src, dst, send, recv, **where):
        return pltpu.make_async_remote_copy(
            src_ref=src, dst_ref=dst, send_sem=send, recv_sem=recv,
            device_id=self.device(**where), device_id_type=MESH,
        )

    def greet(self, wheres):
        barrier = pltpu.get_barrier_semaphore()
        for where in wheres:
            pl.semaphore_signal(
                barrier, inc=1, device_id=self.device(**where), device_id_type=MESH
            )
        return barrier

    def ring_neighbours(self):
        z, y = self.z, self.y
        return [
            dict(z=(z + 1) % NZ), dict(z=(z + NZ - 1) % NZ),
            dict(y=(y + 1) % NY), dict(y=(y + 3) % NY), dict(y=(y + 2) % NY),
            dict(core=1 - self.core),
        ]


QCOLS = HEADS * HD
PIECE = 16
STEPS = 9
TURNS = 12
SPREAD_SEMS = [
    DMA((2,)), DMA((2,)), DMA((3,)), DMA((3,)), DMA((3,)), DMA((3,)),
    DMA((2, STEPS)), DMA((2, STEPS)), DMA((2, STEPS)), DMA((2, STEPS)),
    DMA((2, STEPS)), DMA((2, STEPS)), DMA((2, STEPS)), DMA((2, STEPS)),
]


class Spread:
    def __init__(self, place, one, row, half, sems):
        self.p, self.one, self.row, self.half = place, one, row, half
        (self.w_send, self.w_recv, self.f_send, self.f_recv, self.o_send, self.o_recv,
         self.z_send, self.z_recv,
         self.y_send, self.y_recv, self.h_send, self.h_recv, self.s_send, self.s_recv) = sems
        self.last = 8 - place.core

    def group(self, way, step):
        return (self.p.z + NZ - step + 2 * step * way) % NZ

    def waits(self, ref, sem):
        self.p.copy(ref, ref, self.w_send.at[0], sem, core=1 - self.p.core).wait_recv()

    def z_part(self, part, step):
        p, group = self.p, self.group(self.p.core, step)
        return self.one(0, group, p.y) if part == 0 else self.row(1, group)

    def z_copy(self, part, step):
        p, ref = self.p, self.z_part(part, step)
        return p.copy(ref, ref, self.z_send.at[part, step], self.z_recv.at[part, step + 1],
                      z=(p.z + 17 - 2 * p.core) % NZ)

    def y_copy(self, way, step):
        p = self.p
        ref = self.one(0, self.group(p.core, step), p.y)
        return p.copy(ref, ref, self.y_send.at[way, step], self.y_recv.at[way, step],
                      y=(p.y + 1 + 2 * way) % NY)

    def half_copy(self, way, step):
        p = self.p
        ref = self.half(self.one(0, self.group(p.core, step), (p.y + 3 + 2 * way) % NY), way)
        return p.copy(ref, ref, self.h_send.at[way, step], self.h_recv.at[way, step],
                      y=(p.y + 1 + 2 * way) % NY)

    def first_copy(self, j):
        p, ref = self.p, self.one(1, self.p.z, self.p.y)
        return p.copy(ref, ref, self.f_send.at[j], self.f_recv.at[j], y=(p.y + 1 + j) % NY)

    def sib_copy(self, part, step):
        p = self.p
        ref = self.row(part, self.group(p.core, step))
        return p.copy(ref, ref, self.s_send.at[part, step], self.s_recv.at[part, step],
                      core=1 - p.core)

    def own_copy(self, j):
        p = self.p
        ref = self.one(0, p.z, (p.y + 1 + j) % NY)
        return p.copy(ref, ref, self.o_send.at[j], self.o_recv.at[j], core=1 - p.core)

    def begin(self):
        self.z_copy(0, 0).start()
        for j in range(3):
            self.first_copy(j).start()

        @pl.when(self.p.core == 0)
        def _():
            self.y_copy(0, 0).start()
            self.y_copy(1, 0).start()

    def begin_b(self):
        for j in range(3):
            self.first_copy(j).wait_recv()
        self.z_copy(1, 0).start()

    def along_z(self, step):
        for part in range(2):
            @pl.when(step <= self.last)
            def _():
                self.waits(self.z_part(part, step), self.z_recv.at[part, step])

                @pl.when(step < self.last)
                def _():
                    self.z_copy(part, step).start()

                if part == 0:
                    self.y_copy(0, step).start()
                    self.y_copy(1, step).start()
                else:
                    self.sib_copy(1, step).start()

    def along_y(self, step):
        core = self.p.core

        @pl.when((step - 1 <= self.last) & (step - 1 >= core))
        def _():
            for way in range(2):
                self.y_copy(way, step - 1).wait_recv()
                self.half_copy(way, step - 1).start()

        @pl.when((step - 2 <= self.last) & (step - 2 >= core))
        def _():
            for way in range(2):
                self.half_copy(way, step - 2).wait_recv()

            @pl.when(step > 2)
            def _():
                self.sib_copy(0, step - 2).start()

            @pl.when(step == 2)
            def _():
                for j in range(3):
                    self.own_copy(j).start()

    def own_arrived(self):
        @pl.when(self.p.core == 1)
        def _():
            for j in range(3):
                self.own_copy(j).wait_recv()

    def sib_arrived(self, step):
        group = self.group(1 - self.p.core, step)
        for part in range(2):
            self.waits(self.row(part, group), self.s_recv.at[part, step])

    def settle(self):
        core = self.p.core
        for j in range(3):
            self.first_copy(j).wait_send()

        @pl.when(core == 0)
        def _():
            for j in range(3):
                self.own_copy(j).wait_send()

        def settle_step(step, carry):
            for part in range(2):
                @pl.when(step < self.last)
                def _():
                    self.z_copy(part, step).wait_send()

                @pl.when((step <= self.last) & (step > 0))
                def _():
                    self.sib_copy(part, step).wait_send()

            @pl.when((step <= self.last) & (step >= core))
            def _():
                for way in range(2):
                    self.y_copy(way, step).wait_send()
                    self.half_copy(way, step).wait_send()

            return carry

        lax.fori_loop(0, STEPS, settle_step, 0)


def columns_of(x):
    return (x % 2) * 2 + x // 2


def layer_kernel(
    q_ref, kv_ref, piece_ref, out_ref, buf, w, pieces, heads, top, acc,
    wx_send, wx_recv, ax_send, ax_recv, ah_send, ah_recv, *sems,
):
    p = Place()
    keys_values = Spread(
        p, lambda part, z, y: buf.at[part, z, y], lambda part, z: buf.at[part, z],
        lambda block, way: block.at[pl.ds(way * 64, 64)], sems[:14],
    )
    groups = (pl.ds(0, 3), pl.ds(3, 1))
    halves = (pl.ds(0, 2), pl.ds(2, 1))
    weights = Spread(
        p, lambda part, z, y: w.at[z, y, groups[part]], lambda part, z: w.at[z, :, groups[part]],
        lambda block, way: block.at[halves[way]], sems[14:],
    )
    barrier = p.greet(p.ring_neighbours() + [dict(x=(p.x + j) % 4) for j in (1, 2, 3)])
    top[...] = jnp.full_like(top, -1e30)
    acc[...] = jnp.zeros_like(acc)
    buf[p.core, p.z, p.y] = kv_ref[...]
    pieces[p.x] = piece_ref[columns_of(p.x)]
    pl.semaphore_wait(barrier, 9)

    def kv_swap():
        ref = buf.at[p.core, p.z, p.y]
        return p.copy(ref, ref, keys_values.w_send.at[0], keys_values.w_recv.at[0], core=1 - p.core)

    def w_swap(xl):
        ref = w.at[p.z, p.y, 2 * xl + p.core]
        return p.copy(ref, ref, weights.w_send.at[xl], weights.w_recv.at[xl], core=1 - p.core)

    def piece_copy(j):
        x = (p.x + j) % 4
        return p.copy(piece_ref.at[columns_of(x)], pieces.at[p.x], wx_send.at[j - 1],
                      wx_recv.at[j - 1], x=x)

    def piece_from(j):
        x = (p.x + 4 - j) % 4
        return p.copy(pieces.at[x], pieces.at[x], wx_send.at[j - 1], wx_recv.at[j - 1], x=x)

    kv_swap().start()
    for j in (1, 2, 3):
        piece_copy(j).start()
    keys_values.waits(buf.at[1 - p.core, p.z, p.y], keys_values.w_recv.at[0])
    keys_values.begin()
    for j in (1, 2, 3):
        piece_from(j).wait_recv()
    for xl in range(2):
        w[p.z, p.y, 2 * xl + p.core] = pieces[xl] + pieces[2 + xl]
        w_swap(xl).start()
    keys_values.begin_b()
    for xl in range(2):
        weights.waits(w.at[p.z, p.y, 2 * xl + 1 - p.core], weights.w_recv.at[xl])
    weights.begin()

    def attend(group, masked):
        block = jnp.concatenate(
            [buf[0, group].reshape(NY * BLK, 2 * HD), buf[1, group].reshape(NY * BLK, 2 * HD)], axis=0
        )
        keys = block[:, :HD]
        values = block[:, HD:]
        values = jnp.concatenate([values, jnp.ones_like(values)], axis=1)
        if masked:
            lane = lax.broadcasted_iota(jnp.int32, (BLK, 2 * NY * BLK), 1)
            position = (((lane // BLK) % NY) * 2 + lane // (NY * BLK)) * BLK + lane % BLK
            row = lax.broadcasted_iota(jnp.int32, (BLK, 2 * NY * BLK), 0)
            allowed = position <= (p.y * 2 + p.core) * BLK + row
        for head in range(HEADS):
            rows = pl.ds(head * BLK, BLK)
            scores = lax.dot_general(
                q_ref[:, head * HD:(head + 1) * HD], keys, NT, preferred_element_type=F32
            ) * SCORE_SCALE
            if masked:
                scores = jnp.where(allowed, scores, F32(-1e30))
            old = top[rows, :]
            new = jnp.maximum(old, jnp.max(scores, axis=1, keepdims=True))
            top[rows, :] = new
            shrink = jnp.exp2(old - new)
            expo = jnp.exp2(scores - new[:, :1]).astype(BF)
            added = jnp.dot(expo, values, preferred_element_type=F32)
            acc[rows, :] = acc[rows, :] * jnp.concatenate([shrink, shrink], axis=1) + added

    def turn(step, carry):
        keys_values.along_z(step)
        keys_values.along_y(step)

        @pl.when(step == 1)
        def _():
            weights.begin_b()

        weights.along_z(step)
        weights.along_y(step)

        @pl.when(step == 3)
        def _():
            keys_values.own_arrived()
            attend(p.z, True)
            weights.own_arrived()

        def part(j, carry):
            way = (p.core + j) % 2
            back = step - 2 - j
            here = (back >= 1) & (back <= 8 - way)
            group = keys_values.group(way, back)

            @pl.when(here & (j == 1))
            def _():
                keys_values.sib_arrived(back)
                weights.sib_arrived(back)

            @pl.when(here & (group < p.z))
            def _():
                attend(group, False)

            return carry

        lax.fori_loop(0, 2, part, 0)
        return carry

    lax.fori_loop(1, TURNS, turn, 0)

    depth = NZ * NY * PIECE
    row = lax.broadcasted_iota(jnp.int32, (QCOLS, depth), 0)
    lane = lax.broadcasted_iota(jnp.int32, (QCOLS, depth), 1)
    spot = (lane // PIECE) * (PIECE - 2) + lane % PIECE
    widen = ((row == spot) & (lane % PIECE < PIECE - 2)).astype(F32).astype(BF)
    attended = jnp.concatenate(
        [(acc[pl.ds(head * BLK, BLK), :HD] / acc[pl.ds(head * BLK, BLK), HD:]).astype(BF)
         for head in range(HEADS)], axis=1
    )
    heads[p.x] = jnp.dot(attended, widen, preferred_element_type=F32).astype(BF)

    def heads_copy(way):
        ref = heads.at[p.x]
        return p.copy(ref, ref, ax_send.at[way], ax_recv.at[way], x=(p.x + 1 + 2 * way) % 4)

    def heads_half(way):
        ref = heads.at[(p.x + 3 + 2 * way) % 4, pl.ds(way * 64, 64)]
        return p.copy(ref, ref, ah_send.at[way], ah_recv.at[way], x=(p.x + 1 + 2 * way) % 4)

    def product(x):
        rows = w[:, :, columns_of(x)].reshape(depth, QCOLS)
        return jnp.dot(heads[x], rows, preferred_element_type=F32)

    heads_copy(0).start()
    heads_copy(1).start()
    total = product(p.x)
    for way in range(2):
        heads_copy(way).wait_recv()
        heads_half(way).start()
    total += product((p.x + 3) % 4)
    total += product((p.x + 1) % 4)
    for way in range(2):
        heads_half(way).wait_recv()
    total += product((p.x + 2) % 4)
    out_ref[...] = total.astype(BF)

    kv_swap().wait_send()
    for xl in range(2):
        w_swap(xl).wait_send()
    for j in (1, 2, 3):
        piece_copy(j).wait_send()
    for way in range(2):
        heads_copy(way).wait_send()
        heads_half(way).wait_send()
    keys_values.settle()
    weights.settle()


def layer(queries, keys_values, w_out):
    xh = lax.axis_index("ctx") % 2
    rows = w_out.shape[0]
    piece = jnp.where(
        xh == 0,
        jnp.pad(w_out, ((0, PIECE - rows), (0, 0))),
        jnp.pad(w_out, ((rows, PIECE - 2 * rows), (0, 0))),
    )
    piece = jnp.transpose(piece.reshape(PIECE, 4, QCOLS), (1, 0, 2))
    return pl.pallas_call(
        layer_kernel,
        out_shape=jax.ShapeDtypeStruct((BLK, QCOLS), BF),
        in_specs=[VMEM, VMEM, VMEM],
        out_specs=VMEM,
        scratch_shapes=[
            pltpu.VMEM((2, NZ, NY, BLK, 2 * HD), BF),
            pltpu.VMEM((NZ, NY, 4, PIECE, QCOLS), BF),
            pltpu.VMEM((4, PIECE, QCOLS), BF),
            pltpu.VMEM((4, BLK, NZ * NY * PIECE), BF),
            pltpu.VMEM((HEADS * BLK, HD), F32),
            pltpu.VMEM((HEADS * BLK, 2 * HD), F32),
            DMA((3,)), DMA((3,)), DMA((2,)), DMA((2,)), DMA((2,)), DMA((2,)),
            *SPREAD_SEMS, *SPREAD_SEMS,
        ],
        compiler_params=pltpu.CompilerParams(
            collective_id=0, has_side_effects=True, vmem_limit_bytes=50 * 2**20
        ),
        name="layer",
    )(queries, keys_values, piece)


def swap_core(value):
    pairs = []
    for ctx in range(lax.axis_size("ctx")):
        for tp in range(lax.axis_size("tp")):
            xh, core = ctx % 2, tp % 2
            pairs.append((ctx * 4 + tp, (ctx - xh + core) * 4 + tp - core + xh))
    return lax.ppermute(value, ("ctx", "tp"), pairs)


WIDE = 640


def route_kernel(
    patch_ref, q_ref, kv_ref, slot_ref, source_ref, q_out, kv_out,
    outgoing, near, onward, landed, q_in, kv_in,
    n_send, n_recv, f_send, f_recv, t_send, t_recv,
):
    p = Place()
    straight = p.xh == p.core
    j_me = p.y * 2 + p.xh

    def near_device(i):
        return dict(y=i // 2, x=p.core * 2 + p.xl, core=i % 2)

    def near_source(j):
        return dict(y=j // 2, x=(j % 2) * 2 + p.xl, core=p.xh)

    def is_me(i):
        return straight & (p.y * 2 + p.core == i)

    barrier = pltpu.get_barrier_semaphore()
    for j in range(8):
        @pl.when(jnp.logical_not(is_me(j)))
        def _():
            pl.semaphore_signal(barrier, inc=1, device_id=p.device(**near_source(j)),
                                device_id_type=MESH)
    for i in range(1, NZ):
        pl.semaphore_signal(barrier, inc=1, device_id=p.device(z=(p.z + i) % NZ),
                            device_id_type=MESH)

    lane = lax.broadcasted_iota(jnp.int32, (BLK, patch_ref.shape[0]), 0)
    placing = (lane == slot_ref[...]).astype(F32).astype(BF)
    outgoing[...] = jnp.dot(placing, patch_ref[...], preferred_element_type=F32).astype(BF)

    @pl.when(straight)
    def _():
        pl.semaphore_wait(barrier, 22)

    @pl.when(jnp.logical_not(straight))
    def _():
        pl.semaphore_wait(barrier, 23)

    def near_copy(i):
        return p.copy(outgoing.at[pl.ds(i * NZ, NZ)], near.at[j_me], n_send.at[i], n_recv.at[j_me],
                      **near_device(i))

    def near_arrival(j):
        return p.copy(near.at[j], near.at[j], n_send.at[j], n_recv.at[j], **near_source(j))

    def far_copy(i):
        z = (p.z + i) % NZ
        return p.copy(onward.at[z], landed.at[p.z], f_send.at[i], f_recv.at[p.z], z=z)

    def far_arrival(i):
        z = (p.z + i) % NZ
        return p.copy(landed.at[z], landed.at[z], f_send.at[i], f_recv.at[z], z=z)

    def text_copies():
        to = dict(x=p.core * 2 + p.xl, core=p.xh)
        return (p.copy(q_ref, q_in, t_send.at[0], t_recv.at[0], **to),
                p.copy(kv_ref, kv_in, t_send.at[1], t_recv.at[1], **to))

    for i in range(8):
        @pl.when(jnp.logical_not(is_me(i)))
        def _():
            near_copy(i).start()

        @pl.when(is_me(i))
        def _():
            near[i] = outgoing[i * NZ:(i + 1) * NZ, :]

    @pl.when(jnp.logical_not(straight))
    def _():
        for copy in text_copies():
            copy.start()

    @pl.when(straight)
    def _():
        q_in[...] = q_ref[...]
        kv_in[...] = kv_ref[...]

    for j in range(8):
        @pl.when(jnp.logical_not(is_me(j)))
        def _():
            near_arrival(j).wait_recv()

    held = near[...].reshape(8 * NZ, HEADS * HD + 2 * HD)
    row = lax.broadcasted_iota(jnp.int32, (NZ * 16, 8 * NZ), 0)
    lane = lax.broadcasted_iota(jnp.int32, (NZ * 16, 8 * NZ), 1)
    wanted = (row % 16) // 2 * NZ + row // 16
    second = row % 2 == 1
    zeros = jnp.zeros((8 * NZ, 2 * WIDE - held.shape[1]), BF)
    onward[...] = (
        jnp.dot(((lane == wanted) & jnp.logical_not(second)).astype(F32).astype(BF),
                held[:, :WIDE], preferred_element_type=F32)
        + jnp.dot(((lane == wanted) & second).astype(F32).astype(BF),
                  jnp.concatenate([held[:, WIDE:], zeros], axis=1), preferred_element_type=F32)
    ).astype(BF).reshape(NZ, 16, WIDE)
    order = (8, 7, 9, 6, 10, 5, 11, 4, 12, 3, 13, 2, 14, 1, 15)
    for i in order:
        far_copy(i).start()
    landed[p.z] = onward[p.z]

    @pl.when(jnp.logical_not(straight))
    def _():
        for copy in text_copies():
            copy.wait()

    for i in order:
        far_arrival(i).wait_recv()

    rows = landed[...].reshape(NZ * 16, WIDE)
    source = source_ref[...]
    lane = lax.broadcasted_iota(jnp.int32, (BLK, NZ * 16), 1)
    first = jnp.dot((lane == source * 2).astype(F32).astype(BF), rows, preferred_element_type=F32)
    rest = jnp.dot((lane == source * 2 + 1).astype(F32).astype(BF), rows, preferred_element_type=F32)
    picked = jnp.concatenate([first, rest[:, :q_ref.shape[1] + kv_ref.shape[1] - WIDE]], axis=1)
    is_image = source >= 0
    cut = q_ref.shape[1]
    q_out[...] = jnp.where(is_image, picked[:, :cut], q_in[...].astype(F32)).astype(BF)
    kv_out[...] = jnp.where(is_image, picked[:, cut:], kv_in[...].astype(F32)).astype(BF)

    for i in range(8):
        @pl.when(jnp.logical_not(is_me(i)))
        def _():
            near_copy(i).wait_send()
    for i in order:
        far_copy(i).wait_send()


def route(patch_rows, q_text, kv_text, image_count):
    img_rows = patch_rows.shape[0]
    shards = lax.axis_size("ctx")
    me = lax.axis_index("ctx")
    ends = jnp.cumsum(image_count)
    image_index = me + shards * jnp.arange(img_rows, dtype=jnp.int32)
    target = jnp.sum((ends[None, :] <= image_index[:, None]).astype(jnp.int32), axis=1)
    slot = (target % 8) * NZ + target // 8
    mine = me - me % 2 + lax.axis_index("tp") % 2
    first = BLK - jnp.take(image_count, mine)
    local = jnp.arange(BLK, dtype=jnp.int32)
    index = jnp.take(ends, mine) - BLK + local
    source = jnp.where(local >= first, index % shards, -1)
    return pl.pallas_call(
        route_kernel,
        out_shape=[jax.ShapeDtypeStruct(q_text.shape, BF), jax.ShapeDtypeStruct(kv_text.shape, BF)],
        in_specs=[VMEM] * 5,
        out_specs=[VMEM] * 2,
        scratch_shapes=[
            pltpu.VMEM((BLK, patch_rows.shape[1]), BF),
            pltpu.VMEM((8, NZ, patch_rows.shape[1]), BF),
            pltpu.VMEM((NZ, 16, WIDE), BF), pltpu.VMEM((NZ, 16, WIDE), BF),
            pltpu.VMEM(q_text.shape, BF), pltpu.VMEM(kv_text.shape, BF),
            DMA((8,)), DMA((8,)), DMA((NZ,)), DMA((NZ,)), DMA((2,)), DMA((2,)),
        ],
        compiler_params=pltpu.CompilerParams(
            collective_id=1, has_side_effects=True, vmem_limit_bytes=24 * 2**20
        ),
        name="route",
    )(patch_rows, q_text, kv_text, slot[None, :], source[:, None])


def body(q_text, kv_text, patch_rows, image_count, w_out):
    queries, keys_values = route(patch_rows, q_text, kv_text, image_count)
    return swap_core(layer(queries, keys_values, w_out))


def solution(mesh):
    in_specs = (P("ctx", "tp"), P("ctx", "tp"), P("ctx", "tp"), P(), P(("tp", "ctx"), None))
    out_specs = P("ctx", "tp")
    return jax.shard_map(body, mesh=mesh, in_specs=in_specs, out_specs=out_specs, check_vma=False)
```

```python
import functools

import jax
import jax.numpy as jnp
from jax import lax
from jax.experimental import pallas as pl
from jax.experimental.pallas import tpu as pltpu
from jax.sharding import PartitionSpec as P

HD = 128
HEADS = 7
BLK = 128
NZ, NY = 16, 4
BF = jnp.bfloat16
F32 = jnp.float32
NT = (((1,), (1,)), ((), ()))
SCORE_SCALE = 0.08838834764831845 * 1.4426950408889634
MESH = pl.DeviceIdType.MESH
VMEM = pl.BlockSpec(memory_space=pltpu.VMEM)
DMA = pltpu.SemaphoreType.DMA


class Place:
    def __init__(self):
        ctx = lax.axis_index("ctx")
        tp = lax.axis_index("tp")
        self.z, self.y, self.xh = ctx // 8, (ctx // 2) % 4, ctx % 2
        self.xl, self.core = tp // 2, tp % 2
        self.x = self.xh * 2 + self.xl

    def device(self, z=None, y=None, x=None, core=None):
        z = self.z if z is None else z
        y = self.y if y is None else y
        x = self.x if x is None else x
        core = self.core if core is None else core
        return ((z * 4 + y) * 2 + x // 2, (x % 2) * 2 + core)

    def copy(self, src, dst, send, recv, **where):
        return pltpu.make_async_remote_copy(
            src_ref=src, dst_ref=dst, send_sem=send, recv_sem=recv,
            device_id=self.device(**where), device_id_type=MESH,
        )

    def greet(self, **where):
        pl.semaphore_signal(pltpu.get_barrier_semaphore(), inc=1, device_id=self.device(**where),
                            device_id_type=MESH)


HOPS = 9
ROUNDS = 8
SPREAD_SEMS = [
    DMA((HOPS,)), DMA((HOPS,)), DMA((2, HOPS)), DMA((2, HOPS)), DMA((2, HOPS)), DMA((2, HOPS)),
    DMA((HOPS,)), DMA((HOPS,)), DMA((3,)), DMA((3,)),
]


class Spread:
    def __init__(self, place, everything, half, sems):
        self.p, self.all, self.half = place, everything, half
        (self.z_send, self.z_recv, self.y_send, self.y_recv, self.h_send, self.h_recv,
         self.s_send, self.s_recv, self.o_send, self.o_recv) = sems
        self.last = 8 - place.core

    def group(self, way, hop):
        return (self.p.z + NZ - hop + 2 * hop * way) % NZ

    def mine(self, hop):
        return self.all.at[self.group(self.p.core, hop), self.p.y]

    def waits(self, ref, sem):
        self.p.copy(ref, ref, self.o_send.at[0], sem, core=1 - self.p.core).wait_recv()

    def z_copy(self, hop, far):
        p, ref, end = self.p, self.mine(hop), hop + far
        return p.copy(ref, ref, self.z_send.at[end], self.z_recv.at[end],
                      z=(p.z + NZ + far - 2 * far * p.core) % NZ)

    def z_start(self, hop):
        for far in (2, 1):
            @pl.when(hop + far <= self.last)
            def _():
                self.z_copy(hop, far).start()

    def y_copy(self, way, hop):
        p, ref = self.p, self.mine(hop)
        return p.copy(ref, ref, self.y_send.at[way, hop], self.y_recv.at[way, hop],
                      y=(p.y + 1 + 2 * way) % NY)

    def half_copy(self, way, hop):
        p = self.p
        ref = self.half(self.all.at[self.group(p.core, hop), (p.y + 3 + 2 * way) % NY], way)
        return p.copy(ref, ref, self.h_send.at[way, hop], self.h_recv.at[way, hop],
                      y=(p.y + 1 + 2 * way) % NY)

    def sib_copy(self, hop):
        p = self.p
        ref = self.all.at[self.group(p.core, hop)]
        return p.copy(ref, ref, self.s_send.at[hop], self.s_recv.at[hop], core=1 - p.core)

    def own_copy(self, j):
        p = self.p
        ref = self.all.at[p.z, (p.y + 1 + j) % NY]
        return p.copy(ref, ref, self.o_send.at[j], self.o_recv.at[j], core=1 - p.core)

    def begin(self):
        self.z_start(0)

        @pl.when(self.p.core == 0)
        def _():
            self.y_copy(0, 0).start()
            self.y_copy(1, 0).start()

    def there(self, hop):
        return (hop <= self.last) & (hop >= self.p.core)

    def along_z(self, hop):
        @pl.when(hop <= self.last)
        def _():
            self.waits(self.mine(hop), self.z_recv.at[hop])
            self.z_start(hop)
            self.y_copy(0, hop).start()
            self.y_copy(1, hop).start()

        @pl.when(hop - 1 <= self.last)
        def _():
            self.waits(self.mine(hop - 1), self.z_recv.at[hop - 1])
            self.y_copy(0, hop - 1).start()
            self.y_copy(1, hop - 1).start()

    def across_y(self, hop):
        @pl.when(self.there(hop))
        def _():
            for way in range(2):
                self.y_copy(way, hop).wait_recv()
                self.half_copy(way, hop).start()

    def hand_over(self, hop):
        @pl.when(self.there(hop))
        def _():
            for way in range(2):
                self.half_copy(way, hop).wait_recv()

            @pl.when(hop > 0)
            def _():
                self.sib_copy(hop).start()

            @pl.when(hop == 0)
            def _():
                for j in range(3):
                    self.own_copy(j).start()

    def own_arrived(self):
        @pl.when(self.p.core == 1)
        def _():
            for j in range(3):
                self.own_copy(j).wait_recv()

    def sib_arrived(self, hop):
        self.waits(self.all.at[self.group(1 - self.p.core, hop)], self.s_recv.at[hop])

    def settle(self):
        def settle_hop(hop, carry):
            @pl.when((hop > 0) & (hop <= self.last))
            def _():
                self.waits_sent(hop)
                self.sib_copy(hop).wait_send()

            @pl.when(self.there(hop))
            def _():
                for way in range(2):
                    self.y_copy(way, hop).wait_send()
                    self.half_copy(way, hop).wait_send()

            return carry

        lax.fori_loop(0, HOPS, settle_hop, 0)

        @pl.when(self.p.core == 0)
        def _():
            for j in range(3):
                self.own_copy(j).wait_send()

    def waits_sent(self, end):
        self.z_copy(end - 1, 1).wait_send()

    def round(self, m):
        self.along_z(2 * m)
        for hop in (2 * m - 2, 2 * m - 3):
            @pl.when(hop >= 0)
            def _():
                self.across_y(hop)
        for hop in (2 * m - 4, 2 * m - 5):
            @pl.when(hop >= 0)
            def _():
                self.hand_over(hop)


RING_SEMS = [DMA((3,)), DMA((3,)), DMA((HOPS,)), DMA((HOPS,)), DMA((HOPS,)), DMA((HOPS,))]


class Ring:
    def __init__(self, place, everything, part, sems):
        self.p, self.all, self.part = place, everything, part
        self.f_send, self.f_recv, self.z_send, self.z_recv, self.s_send, self.s_recv = sems
        self.last = 8 - place.core

    def group(self, way, step):
        return self.all.at[(self.p.z + NZ - step + 2 * step * way) % NZ, :, self.part]

    def waits(self, ref, sem):
        self.p.copy(ref, ref, self.f_send.at[0], sem, core=1 - self.p.core).wait_recv()

    def first_copy(self, j):
        p, ref = self.p, self.all.at[self.p.z, self.p.y, self.part]
        return p.copy(ref, ref, self.f_send.at[j], self.f_recv.at[j], y=(p.y + 1 + j) % NY)

    def z_copy(self, step):
        p, ref = self.p, self.group(self.p.core, step)
        return p.copy(ref, ref, self.z_send.at[step], self.z_recv.at[step + 1],
                      z=(p.z + 17 - 2 * p.core) % NZ)

    def sib_copy(self, step):
        p, ref = self.p, self.group(self.p.core, step)
        return p.copy(ref, ref, self.s_send.at[step], self.s_recv.at[step], core=1 - p.core)

    def begin(self):
        for j in range(3):
            self.first_copy(j).start()

    def set_off(self):
        for j in range(3):
            self.first_copy(j).wait_recv()
        self.z_copy(0).start()

    def step(self, step):
        @pl.when(step <= self.last)
        def _():
            self.waits(self.group(self.p.core, step), self.z_recv.at[step])

            @pl.when(step < self.last)
            def _():
                self.z_copy(step).start()

            self.sib_copy(step).start()

    def settle(self):
        for j in range(3):
            self.first_copy(j).wait_send()

        def settle_step(step, carry):
            @pl.when(step < self.last)
            def _():
                self.z_copy(step).wait_send()

            @pl.when((step > 0) & (step <= self.last))
            def _():
                self.sib_copy(step).wait_send()

            return carry

        lax.fori_loop(0, HOPS, settle_step, 0)

    def arrived(self):
        def arrival(step, carry):
            @pl.when(step <= 7 + self.p.core)
            def _():
                self.waits(self.group(1 - self.p.core, step), self.s_recv.at[step])

            return carry

        lax.fori_loop(1, HOPS, arrival, 0)


QCOLS = HEADS * HD
PIECE = 16
WIDE = 640


def columns_of(x):
    return (x % 2) * 2 + x // 2


def layer_kernel(
    patch_hbm, q_ref, kv_ref, count_hbm, w_out_hbm, out_ref,
    patch_ref, count_ref, w_out_ref, piece, outgoing, near, onward, landed, q_in, kv_in, queries,
    buf, w, pieces, heads, top, acc,
    l_sem, n_send, n_recv, f_send, f_recv, t_send, t_recv, c_send, c_recv,
    wx_send, wx_recv, ax_send, ax_recv, ah_send, ah_recv, *sems,
):
    p = Place()
    keys_values = Spread(p, buf, lambda block, way: block.at[way], sems[:10])
    rings = [Ring(p, w, pl.ds(0, 2), sems[10:16]), Ring(p, w, pl.ds(2, 2), sems[16:])]
    straight = p.xh == p.core
    j_me = p.y * 2 + p.xh
    cut = QCOLS

    def near_device(i):
        return dict(y=i // 2, x=p.core * 2 + p.xl, core=i % 2)

    def near_source(j):
        return dict(y=j // 2, x=(j % 2) * 2 + p.xl, core=p.xh)

    def is_me(i):
        return straight & (p.y * 2 + p.core == i)

    loads = [
        pltpu.make_async_copy(count_hbm, count_ref, l_sem.at[0]),
        pltpu.make_async_copy(patch_hbm, patch_ref, l_sem.at[1]),
        pltpu.make_async_copy(w_out_hbm, w_out_ref, l_sem.at[2]),
    ]
    stays = [
        pltpu.make_async_copy(q_ref, q_in, l_sem.at[3]),
        pltpu.make_async_copy(kv_ref, kv_in, l_sem.at[4]),
    ]
    for load in loads:
        load.start()

    @pl.when(straight)
    def _():
        for load in stays:
            load.start()

    for j in range(8):
        @pl.when(jnp.logical_not(is_me(j)))
        def _():
            p.greet(**near_source(j))
    for i in range(1, NZ):
        p.greet(z=(p.z + i) % NZ)
    for i in range(1, 4):
        p.greet(x=(p.x + i) % 4)
    for i in (1, 2, 3):
        p.greet(y=(p.y + i) % NY)
    p.greet(core=1 - p.core)

    for load in loads:
        load.wait()
    filled = w_out_ref.shape[0]
    row = lax.broadcasted_iota(jnp.int32, (PIECE, filled), 0)
    lane = lax.broadcasted_iota(jnp.int32, (PIECE, filled), 1)
    filling = (row == lane + filled * p.xh).astype(F32).astype(BF)
    for b in range(4):
        piece[b] = jnp.dot(filling, w_out_ref[:, b * QCOLS:(b + 1) * QCOLS],
                           preferred_element_type=F32).astype(BF)

    shards = count_ref.shape[1]
    counts = count_ref[...].astype(F32)
    row = lax.broadcasted_iota(jnp.int32, (shards, shards), 0)
    lane = lax.broadcasted_iota(jnp.int32, (shards, shards), 1)
    ends = jnp.sum(jnp.where(lane <= row, counts, F32(0.0)), axis=1, keepdims=True)
    img_rows = patch_ref.shape[0]
    image = (p.z * 4 + p.y) * 2 + p.xh + shards * lax.broadcasted_iota(
        jnp.int32, (shards, img_rows), 1)
    target = jnp.sum(
        jnp.where(ends <= image.astype(F32), F32(1.0), F32(0.0)), axis=0, keepdims=True
    ).astype(jnp.int32)
    slot = (target & 7) * NZ + (target >> 3)
    mine = (p.z * 4 + p.y) * 2 + p.core
    lane = lax.broadcasted_iota(jnp.int32, (1, shards), 1)
    my_count = jnp.sum(jnp.where(lane == mine, counts, F32(0.0)), axis=1, keepdims=True)
    my_end = jnp.sum(jnp.where(lane <= mine, counts, F32(0.0)), axis=1, keepdims=True)
    local = lax.broadcasted_iota(jnp.int32, (BLK, 1), 0)
    source = jnp.where(
        local >= BLK - my_count.astype(jnp.int32),
        (my_end.astype(jnp.int32) + local - BLK) & (shards - 1), -1
    )
    lane = lax.broadcasted_iota(jnp.int32, (BLK, img_rows), 0)
    placing = (lane == slot).astype(F32).astype(BF)
    outgoing[...] = jnp.dot(placing, patch_ref[...], preferred_element_type=F32).astype(BF)

    pieces[p.x] = piece[columns_of(p.x)]
    top[...] = jnp.full_like(top, -1e30)
    acc[...] = jnp.zeros_like(acc)

    @pl.when(straight)
    def _():
        pl.semaphore_wait(pltpu.get_barrier_semaphore(), 29)

    @pl.when(jnp.logical_not(straight))
    def _():
        pl.semaphore_wait(pltpu.get_barrier_semaphore(), 30)

    def near_copy(i):
        return p.copy(outgoing.at[pl.ds(i * NZ, NZ)], near.at[j_me], n_send.at[i], n_recv.at[j_me],
                      **near_device(i))

    def near_arrival(j):
        return p.copy(near.at[j], near.at[j], n_send.at[j], n_recv.at[j], **near_source(j))

    def far_copy(i):
        z = (p.z + i) % NZ
        return p.copy(onward.at[z], landed.at[p.z], f_send.at[i], f_recv.at[p.z], z=z)

    def far_arrival(i):
        z = (p.z + i) % NZ
        return p.copy(landed.at[z], landed.at[z], f_send.at[i], f_recv.at[z], z=z)

    def text_copies():
        to = dict(x=p.core * 2 + p.xl, core=p.xh)
        return (p.copy(q_ref, q_in, t_send.at[0], t_recv.at[0], **to),
                p.copy(kv_ref, kv_in, t_send.at[1], t_recv.at[1], **to))

    def piece_copy(j):
        x = (p.x + j) % 4
        return p.copy(piece.at[columns_of(x)], pieces.at[p.x], wx_send.at[j - 1],
                      wx_recv.at[j - 1], x=x)

    def piece_from(j):
        x = (p.x + 4 - j) % 4
        return p.copy(pieces.at[x], pieces.at[x], wx_send.at[j - 1], wx_recv.at[j - 1], x=x)

    def w_swap(xl):
        ref = w.at[p.z, p.y, 2 * xl + p.core]
        return p.copy(ref, ref, c_send.at[xl], c_recv.at[xl], core=1 - p.core)

    def kv_swap():
        ref = buf.at[p.z, p.y, p.core]
        return p.copy(ref, ref, c_send.at[2], c_recv.at[2], core=1 - p.core)

    for i in range(8):
        @pl.when(jnp.logical_not(is_me(i)))
        def _():
            near_copy(i).start()

        @pl.when(is_me(i))
        def _():
            near[i] = outgoing[i * NZ:(i + 1) * NZ, :]

    @pl.when(jnp.logical_not(straight))
    def _():
        for copy in text_copies():
            copy.start()

    for j in (1, 2, 3):
        piece_copy(j).start()

    for j in range(8):
        @pl.when(jnp.logical_not(is_me(j)))
        def _():
            near_arrival(j).wait_recv()

    held = near[...].reshape(8 * NZ, HEADS * HD + 2 * HD)
    row = lax.broadcasted_iota(jnp.int32, (NZ * 16, 8 * NZ), 0)
    lane = lax.broadcasted_iota(jnp.int32, (NZ * 16, 8 * NZ), 1)
    wanted = (row % 16) // 2 * NZ + row // 16
    second = row % 2 == 1
    zeros = jnp.zeros((8 * NZ, 2 * WIDE - held.shape[1]), BF)
    onward[...] = (
        jnp.dot(((lane == wanted) & jnp.logical_not(second)).astype(F32).astype(BF),
                held[:, :WIDE], preferred_element_type=F32)
        + jnp.dot(((lane == wanted) & second).astype(F32).astype(BF),
                  jnp.concatenate([held[:, WIDE:], zeros], axis=1), preferred_element_type=F32)
    ).astype(BF).reshape(NZ, 16, WIDE)
    order = (8, 7, 9, 6, 10, 5, 11, 4, 12, 3, 13, 2, 14, 1, 15)
    for i in order:
        far_copy(i).start()
    landed[p.z] = onward[p.z]

    for j in (1, 2, 3):
        piece_from(j).wait_recv()
    for xl in range(2):
        w[p.z, p.y, 2 * xl + p.core] = pieces[xl] + pieces[2 + xl]
        w_swap(xl).start()
    for xl in range(2):
        rings[0].waits(w.at[p.z, p.y, 2 * xl + 1 - p.core], c_recv.at[xl])
    for ring in rings:
        ring.begin()

    for ring in rings:
        ring.set_off()
    for ring in rings:
        ring.step(1)

    @pl.when(straight)
    def _():
        for load in stays:
            load.wait()

    @pl.when(jnp.logical_not(straight))
    def _():
        for copy in text_copies():
            copy.wait()

    for i in order:
        far_arrival(i).wait_recv()

    rows = landed[...].reshape(NZ * 16, WIDE)
    lane = lax.broadcasted_iota(jnp.int32, (BLK, NZ * 16), 1)
    first = jnp.dot((lane == source * 2).astype(F32).astype(BF), rows, preferred_element_type=F32)
    rest = jnp.dot((lane == source * 2 + 1).astype(F32).astype(BF), rows, preferred_element_type=F32)
    picked = jnp.concatenate([first, rest[:, :cut + 2 * HD - WIDE]], axis=1)
    is_image = source >= 0
    queries[...] = jnp.where(is_image, picked[:, :cut], q_in[...].astype(F32)).astype(BF)
    buf[p.z, p.y, p.core] = jnp.where(is_image, picked[:, cut:], kv_in[...].astype(F32)).astype(BF)
    kv_swap().start()
    keys_values.waits(buf.at[p.z, p.y, 1 - p.core], c_recv.at[2])
    keys_values.begin()

    def attend(group, masked):
        block = buf[group].reshape(2 * NY * BLK, 2 * HD)
        keys = block[:, :HD]
        values = block[:, HD:]
        values = jnp.concatenate([values, jnp.ones_like(values)], axis=1)
        if masked:
            position = lax.broadcasted_iota(jnp.int32, (BLK, 2 * NY * BLK), 1)
            row = lax.broadcasted_iota(jnp.int32, (BLK, 2 * NY * BLK), 0)
            allowed = position <= (p.y * 2 + p.core) * BLK + row
        for head in range(HEADS):
            rows = pl.ds(head * BLK, BLK)
            scores = lax.dot_general(
                queries[:, head * HD:(head + 1) * HD], keys, NT, preferred_element_type=F32
            ) * SCORE_SCALE
            if masked:
                scores = jnp.where(allowed, scores, F32(-1e30))
            old = top[rows, :]
            new = jnp.maximum(old, jnp.max(scores, axis=1, keepdims=True))
            top[rows, :] = new
            shrink = jnp.exp2(old - new)
            expo = jnp.exp2(scores - new[:, :1]).astype(BF)
            added = jnp.dot(expo, values, preferred_element_type=F32)
            acc[rows, :] = acc[rows, :] * jnp.concatenate([shrink, shrink], axis=1) + added

    def turn(m, carry):
        keys_values.round(m)
        for ring in rings:
            ring.step(m + 1)

        @pl.when(m == 3)
        def _():
            keys_values.own_arrived()
            attend(p.z, True)

        def part(j, carry):
            hop = 2 * m - 4 - j
            way = (p.core + j // 2) % 2
            group = keys_values.group(way, hop)
            here = (hop >= 1) & (hop <= 8 - way)

            @pl.when(here & (j >= 2))
            def _():
                keys_values.sib_arrived(hop)

            @pl.when(here & (group < p.z))
            def _():
                attend(group, False)

            return carry

        lax.fori_loop(0, 4, part, 0)
        return carry

    lax.fori_loop(1, ROUNDS, turn, 0)
    for ring in rings:
        ring.arrived()

    depth = NZ * NY * PIECE
    row = lax.broadcasted_iota(jnp.int32, (QCOLS, depth), 0)
    lane = lax.broadcasted_iota(jnp.int32, (QCOLS, depth), 1)
    spot = (lane // PIECE) * (PIECE - 2) + lane % PIECE
    widen = ((row == spot) & (lane % PIECE < PIECE - 2)).astype(F32).astype(BF)
    attended = jnp.concatenate(
        [(acc[pl.ds(head * BLK, BLK), :HD] / acc[pl.ds(head * BLK, BLK), HD:]).astype(BF)
         for head in range(HEADS)], axis=1
    )
    heads[p.x] = jnp.dot(attended, widen, preferred_element_type=F32).astype(BF)

    def heads_copy(way):
        ref = heads.at[p.x]
        return p.copy(ref, ref, ax_send.at[way], ax_recv.at[way], x=(p.x + 1 + 2 * way) % 4)

    def heads_half(way):
        ref = heads.at[(p.x + 3 + 2 * way) % 4, pl.ds(way * 64, 64)]
        return p.copy(ref, ref, ah_send.at[way], ah_recv.at[way], x=(p.x + 1 + 2 * way) % 4)

    def product(x):
        rows = w[:, :, columns_of(x)].reshape(depth, QCOLS)
        return jnp.dot(heads[x], rows, preferred_element_type=F32)

    heads_copy(0).start()
    heads_copy(1).start()
    total = product(p.x)
    for way in range(2):
        heads_copy(way).wait_recv()
        heads_half(way).start()
    total += product((p.x + 3) % 4)
    total += product((p.x + 1) % 4)
    for way in range(2):
        heads_half(way).wait_recv()
    total += product((p.x + 2) % 4)
    out_ref[...] = total.astype(BF)

    kv_swap().wait_send()
    for xl in range(2):
        w_swap(xl).wait_send()
    for j in (1, 2, 3):
        piece_copy(j).wait_send()
    for way in range(2):
        heads_copy(way).wait_send()
        heads_half(way).wait_send()
    keys_values.settle()
    for ring in rings:
        ring.settle()
    for i in range(8):
        @pl.when(jnp.logical_not(is_me(i)))
        def _():
            near_copy(i).wait_send()
    for i in order:
        far_copy(i).wait_send()


def layer(q_text, kv_text, patch_rows, image_count, w_out):
    width = patch_rows.shape[1]
    return pl.pallas_call(
        layer_kernel,
        out_shape=jax.ShapeDtypeStruct((BLK, QCOLS), BF),
        in_specs=[pl.BlockSpec(memory_space=pltpu.HBM)] * 5,
        out_specs=VMEM,
        scratch_shapes=[
            pltpu.VMEM(patch_rows.shape, BF), pltpu.VMEM((1, image_count.shape[0]), jnp.int32),
            pltpu.VMEM(w_out.shape, BF),
            pltpu.VMEM((4, PIECE, QCOLS), BF),
            pltpu.VMEM((BLK, width), BF),
            pltpu.VMEM((8, NZ, width), BF),
            pltpu.VMEM((NZ, 16, WIDE), BF), pltpu.VMEM((NZ, 16, WIDE), BF),
            pltpu.VMEM(q_text.shape, BF), pltpu.VMEM(kv_text.shape, BF),
            pltpu.VMEM(q_text.shape, BF),
            pltpu.VMEM((NZ, NY, 2, BLK, 2 * HD), BF),
            pltpu.VMEM((NZ, NY, 4, PIECE, QCOLS), BF),
            pltpu.VMEM((4, PIECE, QCOLS), BF),
            pltpu.VMEM((4, BLK, NZ * NY * PIECE), BF),
            pltpu.VMEM((HEADS * BLK, HD), F32),
            pltpu.VMEM((HEADS * BLK, 2 * HD), F32),
            DMA((5,)), DMA((8,)), DMA((8,)), DMA((NZ,)), DMA((NZ,)), DMA((2,)), DMA((2,)),
            DMA((3,)), DMA((3,)),
            DMA((3,)), DMA((3,)), DMA((2,)), DMA((2,)), DMA((2,)), DMA((2,)),
            *SPREAD_SEMS, *RING_SEMS, *RING_SEMS,
        ],
        compiler_params=pltpu.CompilerParams(
            collective_id=0, has_side_effects=True, vmem_limit_bytes=63 * 2**20
        ),
        name="layer",
    )(patch_rows, q_text, kv_text, image_count[None, :], w_out)


def swap_core(value):
    pairs = []
    for ctx in range(lax.axis_size("ctx")):
        for tp in range(lax.axis_size("tp")):
            xh, core = ctx % 2, tp % 2
            pairs.append((ctx * 4 + tp, (ctx - xh + core) * 4 + tp - core + xh))
    return lax.ppermute(value, ("ctx", "tp"), pairs)


def body(q_text, kv_text, patch_rows, image_count, w_out):
    return swap_core(layer(q_text, kv_text, patch_rows, image_count, w_out))


def solution(mesh):
    in_specs = (P("ctx", "tp"), P("ctx", "tp"), P("ctx", "tp"), P(), P(("tp", "ctx"), None))
    out_specs = P("ctx", "tp")
    return jax.shard_map(body, mesh=mesh, in_specs=in_specs, out_specs=out_specs, check_vma=False)
```

```python
import functools

import jax
import jax.numpy as jnp
from jax import lax
from jax.experimental import pallas as pl
from jax.experimental.pallas import tpu as pltpu
from jax.sharding import PartitionSpec as P

HD = 128
HEADS = 7
BLK = 128
NZ, NY = 16, 4
BF = jnp.bfloat16
F32 = jnp.float32
NT = (((1,), (1,)), ((), ()))
SCORE_SCALE = 0.08838834764831845 * 1.4426950408889634
MESH = pl.DeviceIdType.MESH
VMEM = pl.BlockSpec(memory_space=pltpu.VMEM)
DMA = pltpu.SemaphoreType.DMA


class Place:
    def __init__(self):
        ctx = lax.axis_index("ctx")
        tp = lax.axis_index("tp")
        self.z, self.y, self.xh = ctx // 8, (ctx // 2) % 4, ctx % 2
        self.xl, self.core = tp // 2, tp % 2
        self.x = self.xh * 2 + self.xl

    def device(self, z=None, y=None, x=None, core=None):
        z = self.z if z is None else z
        y = self.y if y is None else y
        x = self.x if x is None else x
        core = self.core if core is None else core
        return ((z * 4 + y) * 2 + x // 2, (x % 2) * 2 + core)

    def copy(self, src, dst, send, recv, **where):
        return pltpu.make_async_remote_copy(
            src_ref=src, dst_ref=dst, send_sem=send, recv_sem=recv,
            device_id=self.device(**where), device_id_type=MESH,
        )

    def greet(self, **where):
        pl.semaphore_signal(pltpu.get_barrier_semaphore(), inc=1, device_id=self.device(**where),
                            device_id_type=MESH)


HOPS = 9
ROUNDS = 8
SPREAD_SEMS = [
    DMA((HOPS,)), DMA((HOPS,)), DMA((2, HOPS)), DMA((2, HOPS)), DMA((2, HOPS)), DMA((2, HOPS)),
    DMA((HOPS,)), DMA((HOPS,)), DMA((3,)), DMA((3,)),
]


class Spread:
    def __init__(self, place, everything, half, sems):
        self.p, self.all, self.half = place, everything, half
        (self.z_send, self.z_recv, self.y_send, self.y_recv, self.h_send, self.h_recv,
         self.s_send, self.s_recv, self.o_send, self.o_recv) = sems
        self.last = 8 - place.core

    def group(self, way, hop):
        return (self.p.z + NZ - hop + 2 * hop * way) % NZ

    def mine(self, hop):
        return self.all.at[self.group(self.p.core, hop), self.p.y]

    def waits(self, ref, sem):
        self.p.copy(ref, ref, self.o_send.at[0], sem, core=1 - self.p.core).wait_recv()

    def z_copy(self, hop, far):
        p, ref, end = self.p, self.mine(hop), hop + far
        return p.copy(ref, ref, self.z_send.at[end], self.z_recv.at[end],
                      z=(p.z + NZ + far - 2 * far * p.core) % NZ)

    def z_start(self, hop):
        for far in (2, 1):
            @pl.when(hop + far <= self.last)
            def _():
                self.z_copy(hop, far).start()

    def y_copy(self, way, hop):
        p, ref = self.p, self.mine(hop)
        return p.copy(ref, ref, self.y_send.at[way, hop], self.y_recv.at[way, hop],
                      y=(p.y + 1 + 2 * way) % NY)

    def half_copy(self, way, hop):
        p = self.p
        ref = self.half(self.all.at[self.group(p.core, hop), (p.y + 3 + 2 * way) % NY], way)
        return p.copy(ref, ref, self.h_send.at[way, hop], self.h_recv.at[way, hop],
                      y=(p.y + 1 + 2 * way) % NY)

    def sib_copy(self, hop):
        p = self.p
        ref = self.all.at[self.group(p.core, hop)]
        return p.copy(ref, ref, self.s_send.at[hop], self.s_recv.at[hop], core=1 - p.core)

    def own_copy(self, j):
        p = self.p
        ref = self.all.at[p.z, (p.y + 1 + j) % NY]
        return p.copy(ref, ref, self.o_send.at[j], self.o_recv.at[j], core=1 - p.core)

    def begin(self):
        self.z_start(0)

        @pl.when(self.p.core == 0)
        def _():
            self.y_copy(0, 0).start()
            self.y_copy(1, 0).start()

    def there(self, hop):
        return (hop <= self.last) & (hop >= self.p.core)

    def along_z(self, hop):
        @pl.when(hop <= self.last)
        def _():
            self.waits(self.mine(hop), self.z_recv.at[hop])
            self.z_start(hop)
            self.y_copy(0, hop).start()
            self.y_copy(1, hop).start()

        @pl.when(hop - 1 <= self.last)
        def _():
            self.waits(self.mine(hop - 1), self.z_recv.at[hop - 1])
            self.y_copy(0, hop - 1).start()
            self.y_copy(1, hop - 1).start()

    def across_y(self, hop):
        @pl.when(self.there(hop))
        def _():
            for way in range(2):
                self.y_copy(way, hop).wait_recv()
                self.half_copy(way, hop).start()

    def hand_over(self, hop):
        @pl.when(self.there(hop))
        def _():
            for way in range(2):
                self.half_copy(way, hop).wait_recv()

            @pl.when(hop > 0)
            def _():
                self.sib_copy(hop).start()

            @pl.when(hop == 0)
            def _():
                for j in range(3):
                    self.own_copy(j).start()

    def own_arrived(self):
        @pl.when(self.p.core == 1)
        def _():
            for j in range(3):
                self.own_copy(j).wait_recv()

    def sib_arrived(self, hop):
        self.waits(self.all.at[self.group(1 - self.p.core, hop)], self.s_recv.at[hop])

    def settle(self):
        def settle_hop(hop, carry):
            @pl.when((hop > 0) & (hop <= self.last))
            def _():
                self.waits_sent(hop)
                self.sib_copy(hop).wait_send()

            @pl.when(self.there(hop))
            def _():
                for way in range(2):
                    self.y_copy(way, hop).wait_send()
                    self.half_copy(way, hop).wait_send()

            return carry

        lax.fori_loop(0, HOPS, settle_hop, 0)

        @pl.when(self.p.core == 0)
        def _():
            for j in range(3):
                self.own_copy(j).wait_send()

    def waits_sent(self, end):
        self.z_copy(end - 1, 1).wait_send()

    def round(self, m):
        self.along_z(2 * m)
        for hop in (2 * m - 2, 2 * m - 3):
            @pl.when(hop >= 0)
            def _():
                self.across_y(hop)
        for hop in (2 * m - 4, 2 * m - 5):
            @pl.when(hop >= 0)
            def _():
                self.hand_over(hop)


RING_SEMS = [DMA((3,)), DMA((3,)), DMA((HOPS,)), DMA((HOPS,)), DMA((HOPS,)), DMA((HOPS,))]


class Ring:
    def __init__(self, place, everything, part, sems):
        self.p, self.all, self.part = place, everything, part
        self.f_send, self.f_recv, self.z_send, self.z_recv, self.s_send, self.s_recv = sems
        self.last = 8 - place.core

    def group(self, way, step):
        return self.all.at[(self.p.z + NZ - step + 2 * step * way) % NZ, :, self.part]

    def waits(self, ref, sem):
        self.p.copy(ref, ref, self.f_send.at[0], sem, core=1 - self.p.core).wait_recv()

    def first_copy(self, j):
        p, ref = self.p, self.all.at[self.p.z, self.p.y, self.part]
        return p.copy(ref, ref, self.f_send.at[j], self.f_recv.at[j], y=(p.y + 1 + j) % NY)

    def z_copy(self, step):
        p, ref = self.p, self.group(self.p.core, step)
        return p.copy(ref, ref, self.z_send.at[step], self.z_recv.at[step + 1],
                      z=(p.z + 17 - 2 * p.core) % NZ)

    def sib_copy(self, step):
        p, ref = self.p, self.group(self.p.core, step)
        return p.copy(ref, ref, self.s_send.at[step], self.s_recv.at[step], core=1 - p.core)

    def begin(self):
        for j in range(3):
            self.first_copy(j).start()

    def set_off(self):
        for j in range(3):
            self.first_copy(j).wait_recv()
        self.z_copy(0).start()

    def step(self, step):
        @pl.when(step <= self.last)
        def _():
            self.waits(self.group(self.p.core, step), self.z_recv.at[step])

            @pl.when(step < self.last)
            def _():
                self.z_copy(step).start()

            self.sib_copy(step).start()

    def settle(self):
        for j in range(3):
            self.first_copy(j).wait_send()

        def settle_step(step, carry):
            @pl.when(step < self.last)
            def _():
                self.z_copy(step).wait_send()

            @pl.when((step > 0) & (step <= self.last))
            def _():
                self.sib_copy(step).wait_send()

            return carry

        lax.fori_loop(0, HOPS, settle_step, 0)

    def arrived(self):
        def arrival(step, carry):
            @pl.when(step <= 7 + self.p.core)
            def _():
                self.waits(self.group(1 - self.p.core, step), self.s_recv.at[step])

            return carry

        lax.fori_loop(1, HOPS, arrival, 0)


QCOLS = HEADS * HD
PIECE = 16
WIDE = 640


def columns_of(x):
    return (x % 2) * 2 + x // 2


def layer_kernel(
    patch_hbm, q_ref, kv_ref, count_hbm, w_out_hbm, out_ref,
    patch_ref, count_ref, w_out_ref, piece, outgoing, near, onward, landed, q_in, kv_in, queries,
    buf, w, pieces, heads, widen, result, top, acc,
    l_sem, n_send, n_recv, f_send, f_recv, t_send, t_recv, c_send, c_recv,
    wx_send, wx_recv, ax_send, ax_recv, ah_send, ah_recv, r_send, r_recv, *sems,
):
    p = Place()
    keys_values = Spread(p, buf, lambda block, way: block.at[way], sems[:10])
    rings = [Ring(p, w, pl.ds(0, 2), sems[10:16]), Ring(p, w, pl.ds(2, 2), sems[16:])]
    straight = p.xh == p.core
    j_me = p.y * 2 + p.xh
    cut = QCOLS

    def near_device(i):
        return dict(y=i // 2, x=p.core * 2 + p.xl, core=i % 2)

    def near_source(j):
        return dict(y=j // 2, x=(j % 2) * 2 + p.xl, core=p.xh)

    def is_me(i):
        return straight & (p.y * 2 + p.core == i)

    loads = [
        pltpu.make_async_copy(count_hbm, count_ref, l_sem.at[0]),
        pltpu.make_async_copy(patch_hbm, patch_ref, l_sem.at[1]),
        pltpu.make_async_copy(w_out_hbm, w_out_ref, l_sem.at[2]),
    ]
    stays = [
        pltpu.make_async_copy(q_ref, q_in, l_sem.at[3]),
        pltpu.make_async_copy(kv_ref, kv_in, l_sem.at[4]),
    ]
    for load in loads:
        load.start()

    @pl.when(straight)
    def _():
        for load in stays:
            load.start()

    for j in range(8):
        @pl.when(jnp.logical_not(is_me(j)))
        def _():
            p.greet(**near_source(j))
    for i in range(1, NZ):
        p.greet(z=(p.z + i) % NZ)
    for i in range(1, 4):
        p.greet(x=(p.x + i) % 4)
    for i in (1, 2, 3):
        p.greet(y=(p.y + i) % NY)
    p.greet(core=1 - p.core)

    for load in loads:
        load.wait()
    filled = w_out_ref.shape[0]
    row = lax.broadcasted_iota(jnp.int32, (PIECE, filled), 0)
    lane = lax.broadcasted_iota(jnp.int32, (PIECE, filled), 1)
    filling = (row == lane + filled * p.xh).astype(F32).astype(BF)
    for b in range(4):
        piece[b] = jnp.dot(filling, w_out_ref[:, b * QCOLS:(b + 1) * QCOLS],
                           preferred_element_type=F32).astype(BF)

    shards = count_ref.shape[1]
    counts = count_ref[...].astype(F32)
    row = lax.broadcasted_iota(jnp.int32, (shards, shards), 0)
    lane = lax.broadcasted_iota(jnp.int32, (shards, shards), 1)
    ends = jnp.sum(jnp.where(lane <= row, counts, F32(0.0)), axis=1, keepdims=True)
    img_rows = patch_ref.shape[0]
    image = (p.z * 4 + p.y) * 2 + p.xh + shards * lax.broadcasted_iota(
        jnp.int32, (shards, img_rows), 1)
    target = jnp.sum(
        jnp.where(ends <= image.astype(F32), F32(1.0), F32(0.0)), axis=0, keepdims=True
    ).astype(jnp.int32)
    slot = (target & 7) * NZ + (target >> 3)
    mine = (p.z * 4 + p.y) * 2 + p.core
    lane = lax.broadcasted_iota(jnp.int32, (1, shards), 1)
    my_count = jnp.sum(jnp.where(lane == mine, counts, F32(0.0)), axis=1, keepdims=True)
    my_end = jnp.sum(jnp.where(lane <= mine, counts, F32(0.0)), axis=1, keepdims=True)
    local = lax.broadcasted_iota(jnp.int32, (BLK, 1), 0)
    source = jnp.where(
        local >= BLK - my_count.astype(jnp.int32),
        (my_end.astype(jnp.int32) + local - BLK) & (shards - 1), -1
    )
    lane = lax.broadcasted_iota(jnp.int32, (BLK, img_rows), 0)
    placing = (lane == slot).astype(F32).astype(BF)
    outgoing[...] = jnp.dot(placing, patch_ref[...], preferred_element_type=F32).astype(BF)

    pieces[p.x] = piece[columns_of(p.x)]
    depth = NZ * NY * PIECE
    row = lax.broadcasted_iota(jnp.int32, (QCOLS, depth), 0)
    lane = lax.broadcasted_iota(jnp.int32, (QCOLS, depth), 1)
    spot = (lane // PIECE) * (PIECE - 2) + lane % PIECE
    widen[...] = ((row == spot) & (lane % PIECE < PIECE - 2)).astype(F32).astype(BF)
    top[...] = jnp.full_like(top, -1e30)
    acc[...] = jnp.zeros_like(acc)

    @pl.when(straight)
    def _():
        pl.semaphore_wait(pltpu.get_barrier_semaphore(), 29)

    @pl.when(jnp.logical_not(straight))
    def _():
        pl.semaphore_wait(pltpu.get_barrier_semaphore(), 30)

    def near_copy(i):
        return p.copy(outgoing.at[pl.ds(i * NZ, NZ)], near.at[j_me], n_send.at[i], n_recv.at[j_me],
                      **near_device(i))

    def near_arrival(j):
        return p.copy(near.at[j], near.at[j], n_send.at[j], n_recv.at[j], **near_source(j))

    def far_copy(i):
        z = (p.z + i) % NZ
        return p.copy(onward.at[z], landed.at[p.z], f_send.at[i], f_recv.at[p.z], z=z)

    def far_arrival(i):
        z = (p.z + i) % NZ
        return p.copy(landed.at[z], landed.at[z], f_send.at[i], f_recv.at[z], z=z)

    def text_copies():
        to = dict(x=p.core * 2 + p.xl, core=p.xh)
        return (p.copy(q_ref, q_in, t_send.at[0], t_recv.at[0], **to),
                p.copy(kv_ref, kv_in, t_send.at[1], t_recv.at[1], **to))

    def piece_copy(j):
        x = (p.x + j) % 4
        return p.copy(piece.at[columns_of(x)], pieces.at[p.x], wx_send.at[j - 1],
                      wx_recv.at[j - 1], x=x)

    def piece_from(j):
        x = (p.x + 4 - j) % 4
        return p.copy(pieces.at[x], pieces.at[x], wx_send.at[j - 1], wx_recv.at[j - 1], x=x)

    def w_swap(xl):
        ref = w.at[p.z, p.y, 2 * xl + p.core]
        return p.copy(ref, ref, c_send.at[xl], c_recv.at[xl], core=1 - p.core)

    def kv_swap():
        ref = buf.at[p.z, p.y, p.core]
        return p.copy(ref, ref, c_send.at[2], c_recv.at[2], core=1 - p.core)

    for i in range(8):
        @pl.when(jnp.logical_not(is_me(i)))
        def _():
            near_copy(i).start()

        @pl.when(is_me(i))
        def _():
            near[i] = outgoing[i * NZ:(i + 1) * NZ, :]

    @pl.when(jnp.logical_not(straight))
    def _():
        for copy in text_copies():
            copy.start()

    for j in (1, 2, 3):
        piece_copy(j).start()

    for j in range(8):
        @pl.when(jnp.logical_not(is_me(j)))
        def _():
            near_arrival(j).wait_recv()

    held = near[...].reshape(8 * NZ, HEADS * HD + 2 * HD)
    row = lax.broadcasted_iota(jnp.int32, (NZ * 16, 8 * NZ), 0)
    lane = lax.broadcasted_iota(jnp.int32, (NZ * 16, 8 * NZ), 1)
    wanted = (row % 16) // 2 * NZ + row // 16
    second = row % 2 == 1
    zeros = jnp.zeros((8 * NZ, 2 * WIDE - held.shape[1]), BF)
    onward[...] = (
        jnp.dot(((lane == wanted) & jnp.logical_not(second)).astype(F32).astype(BF),
                held[:, :WIDE], preferred_element_type=F32)
        + jnp.dot(((lane == wanted) & second).astype(F32).astype(BF),
                  jnp.concatenate([held[:, WIDE:], zeros], axis=1), preferred_element_type=F32)
    ).astype(BF).reshape(NZ, 16, WIDE)
    order = (8, 7, 9, 6, 10, 5, 11, 4, 12, 3, 13, 2, 14, 1, 15)
    for i in order:
        far_copy(i).start()
    landed[p.z] = onward[p.z]

    for j in (1, 2, 3):
        piece_from(j).wait_recv()
    for xl in range(2):
        w[p.z, p.y, 2 * xl + p.core] = pieces[xl] + pieces[2 + xl]
        w_swap(xl).start()
    for xl in range(2):
        rings[0].waits(w.at[p.z, p.y, 2 * xl + 1 - p.core], c_recv.at[xl])
    for ring in rings:
        ring.begin()

    for ring in rings:
        ring.set_off()
    for ring in rings:
        ring.step(1)

    @pl.when(straight)
    def _():
        for load in stays:
            load.wait()

    @pl.when(jnp.logical_not(straight))
    def _():
        for copy in text_copies():
            copy.wait()

    for i in order:
        far_arrival(i).wait_recv()

    rows = landed[...].reshape(NZ * 16, WIDE)
    lane = lax.broadcasted_iota(jnp.int32, (BLK, NZ * 16), 1)
    first = jnp.dot((lane == source * 2).astype(F32).astype(BF), rows, preferred_element_type=F32)
    rest = jnp.dot((lane == source * 2 + 1).astype(F32).astype(BF), rows, preferred_element_type=F32)
    picked = jnp.concatenate([first, rest[:, :cut + 2 * HD - WIDE]], axis=1)
    is_image = source >= 0
    queries[...] = jnp.where(is_image, picked[:, :cut], q_in[...].astype(F32)).astype(BF)
    buf[p.z, p.y, p.core] = jnp.where(is_image, picked[:, cut:], kv_in[...].astype(F32)).astype(BF)
    kv_swap().start()
    keys_values.waits(buf.at[p.z, p.y, 1 - p.core], c_recv.at[2])
    keys_values.begin()

    def attend(group, masked):
        block = buf[group].reshape(2 * NY * BLK, 2 * HD)
        keys = block[:, :HD]
        values = block[:, HD:]
        values = jnp.concatenate([values, jnp.ones_like(values)], axis=1)
        if masked:
            position = lax.broadcasted_iota(jnp.int32, (BLK, 2 * NY * BLK), 1)
            row = lax.broadcasted_iota(jnp.int32, (BLK, 2 * NY * BLK), 0)
            allowed = position <= (p.y * 2 + p.core) * BLK + row
        for head in range(HEADS):
            rows = pl.ds(head * BLK, BLK)
            scores = lax.dot_general(
                queries[:, head * HD:(head + 1) * HD], keys, NT, preferred_element_type=F32
            ) * SCORE_SCALE
            if masked:
                scores = jnp.where(allowed, scores, F32(-1e30))
            old = top[rows, :]
            new = jnp.maximum(old, jnp.max(scores, axis=1, keepdims=True))
            top[rows, :] = new
            shrink = jnp.exp2(old - new)
            expo = jnp.exp2(scores - new[:, :1]).astype(BF)
            added = jnp.dot(expo, values, preferred_element_type=F32)
            acc[rows, :] = acc[rows, :] * jnp.concatenate([shrink, shrink], axis=1) + added

    def turn(m, carry):
        keys_values.round(m)
        for ring in rings:
            ring.step(m + 1)

        @pl.when(m == 3)
        def _():
            keys_values.own_arrived()
            attend(p.z, True)

        def part(j, carry):
            hop = 2 * m - 4 - j
            way = (p.core + j // 2) % 2
            group = keys_values.group(way, hop)
            here = (hop >= 1) & (hop <= 8 - way)

            @pl.when(here & (j >= 2))
            def _():
                keys_values.sib_arrived(hop)

            @pl.when(here & (group < p.z))
            def _():
                attend(group, False)

            return carry

        lax.fori_loop(0, 4, part, 0)
        return carry

    lax.fori_loop(1, ROUNDS, turn, 0)
    for ring in rings:
        ring.arrived()

    attended = jnp.concatenate(
        [(acc[pl.ds(head * BLK, BLK), :HD] / acc[pl.ds(head * BLK, BLK), HD:]).astype(BF)
         for head in range(HEADS)], axis=1
    )
    heads[p.x] = jnp.dot(attended, widen[...], preferred_element_type=F32).astype(BF)

    def heads_copy(way, j):
        ref = heads.at[p.x, pl.ds((way + j) % 2 * 64, 64)]
        return p.copy(ref, ref, ax_send.at[way, j], ax_recv.at[way, j], x=(p.x + 1 + 2 * way) % 4)

    def heads_half(way):
        ref = heads.at[(p.x + 3 + 2 * way) % 4, pl.ds(way * 64, 64)]
        return p.copy(ref, ref, ah_send.at[way], ah_recv.at[way], x=(p.x + 1 + 2 * way) % 4)

    def product(x):
        rows = w[:, :, columns_of(x)].reshape(depth, QCOLS)
        return jnp.dot(heads[x], rows, preferred_element_type=F32)

    for j in range(2):
        heads_copy(0, j).start()
        heads_copy(1, j).start()
    total = product(p.x)
    for way in range(2):
        heads_copy(way, 0).wait_recv()
        heads_half(way).start()
    for way in range(2):
        heads_copy(way, 1).wait_recv()
    total += product((p.x + 3) % 4)
    total += product((p.x + 1) % 4)
    for way in range(2):
        heads_half(way).wait_recv()
    total += product((p.x + 2) % 4)
    result[...] = total.astype(BF)
    result_copy = p.copy(result, out_ref, r_send, r_recv, x=p.core * 2 + p.xl, core=p.xh)

    @pl.when(straight)
    def _():
        out_ref[...] = result[...]

    @pl.when(jnp.logical_not(straight))
    def _():
        result_copy.start()


    kv_swap().wait_send()
    for xl in range(2):
        w_swap(xl).wait_send()
    for j in (1, 2, 3):
        piece_copy(j).wait_send()
    for way in range(2):
        heads_copy(way, 0).wait_send()
        heads_copy(way, 1).wait_send()
        heads_half(way).wait_send()
    keys_values.settle()
    for ring in rings:
        ring.settle()
    for i in range(8):
        @pl.when(jnp.logical_not(is_me(i)))
        def _():
            near_copy(i).wait_send()
    for i in order:
        far_copy(i).wait_send()

    @pl.when(jnp.logical_not(straight))
    def _():
        result_copy.wait()


def layer(q_text, kv_text, patch_rows, image_count, w_out):
    width = patch_rows.shape[1]
    return pl.pallas_call(
        layer_kernel,
        out_shape=jax.ShapeDtypeStruct((BLK, QCOLS), BF),
        in_specs=[pl.BlockSpec(memory_space=pltpu.HBM)] * 5,
        out_specs=VMEM,
        scratch_shapes=[
            pltpu.VMEM(patch_rows.shape, BF), pltpu.VMEM((1, image_count.shape[0]), jnp.int32),
            pltpu.VMEM(w_out.shape, BF),
            pltpu.VMEM((4, PIECE, QCOLS), BF),
            pltpu.VMEM((BLK, width), BF),
            pltpu.VMEM((8, NZ, width), BF),
            pltpu.VMEM((NZ, 16, WIDE), BF), pltpu.VMEM((NZ, 16, WIDE), BF),
            pltpu.VMEM(q_text.shape, BF), pltpu.VMEM(kv_text.shape, BF),
            pltpu.VMEM(q_text.shape, BF),
            pltpu.VMEM((NZ, NY, 2, BLK, 2 * HD), BF),
            pltpu.VMEM((NZ, NY, 4, PIECE, QCOLS), BF),
            pltpu.VMEM((4, PIECE, QCOLS), BF),
            pltpu.VMEM((4, BLK, NZ * NY * PIECE), BF),
            pltpu.VMEM((QCOLS, NZ * NY * PIECE), BF),
            pltpu.VMEM((BLK, QCOLS), BF),
            pltpu.VMEM((HEADS * BLK, HD), F32),
            pltpu.VMEM((HEADS * BLK, 2 * HD), F32),
            DMA((5,)), DMA((8,)), DMA((8,)), DMA((NZ,)), DMA((NZ,)), DMA((2,)), DMA((2,)),
            DMA((3,)), DMA((3,)),
            DMA((3,)), DMA((3,)), DMA((2, 2)), DMA((2, 2)), DMA((2,)), DMA((2,)), DMA, DMA,
            *SPREAD_SEMS, *RING_SEMS, *RING_SEMS,
        ],
        compiler_params=pltpu.CompilerParams(
            collective_id=0, has_side_effects=True, vmem_limit_bytes=63 * 2**20
        ),
        name="layer",
    )(patch_rows, q_text, kv_text, image_count[None, :], w_out)


def body(q_text, kv_text, patch_rows, image_count, w_out):
    return layer(q_text, kv_text, patch_rows, image_count, w_out)


def solution(mesh):
    in_specs = (P("ctx", "tp"), P("ctx", "tp"), P("ctx", "tp"), P(), P(("tp", "ctx"), None))
    out_specs = P("ctx", "tp")
    return jax.shard_map(body, mesh=mesh, in_specs=in_specs, out_specs=out_specs, check_vma=False)
```

```python
import functools

import jax
import jax.numpy as jnp
from jax import lax
from jax.experimental import pallas as pl
from jax.experimental.pallas import tpu as pltpu
from jax.sharding import PartitionSpec as P

HD = 128
HEADS = 7
BLK = 128
NZ, NY = 16, 4
BF = jnp.bfloat16
F32 = jnp.float32
NT = (((1,), (1,)), ((), ()))
SCORE_SCALE = 0.08838834764831845 * 1.4426950408889634
MESH = pl.DeviceIdType.MESH
VMEM = pl.BlockSpec(memory_space=pltpu.VMEM)
DMA = pltpu.SemaphoreType.DMA


class Place:
    def __init__(self):
        ctx = lax.axis_index("ctx")
        tp = lax.axis_index("tp")
        self.z, self.y, self.xh = ctx // 8, (ctx // 2) % 4, ctx % 2
        self.xl, self.core = tp // 2, tp % 2
        self.x = self.xh * 2 + self.xl

    def device(self, z=None, y=None, x=None, core=None):
        z = self.z if z is None else z
        y = self.y if y is None else y
        x = self.x if x is None else x
        core = self.core if core is None else core
        return ((z * 4 + y) * 2 + x // 2, (x % 2) * 2 + core)

    def copy(self, src, dst, send, recv, **where):
        return pltpu.make_async_remote_copy(
            src_ref=src, dst_ref=dst, send_sem=send, recv_sem=recv,
            device_id=self.device(**where), device_id_type=MESH,
        )

    def greet(self, **where):
        pl.semaphore_signal(pltpu.get_barrier_semaphore(), inc=1, device_id=self.device(**where),
                            device_id_type=MESH)


HOPS = 9
ROUNDS = 8
SPREAD_SEMS = [
    DMA((HOPS,)), DMA((HOPS,)), DMA((2, HOPS)), DMA((2, HOPS)), DMA((2, HOPS)), DMA((2, HOPS)),
    DMA((HOPS,)), DMA((HOPS,)), DMA((3,)), DMA((3,)),
]


class Spread:
    def __init__(self, place, everything, half, sems):
        self.p, self.all, self.half = place, everything, half
        (self.z_send, self.z_recv, self.y_send, self.y_recv, self.h_send, self.h_recv,
         self.s_send, self.s_recv, self.o_send, self.o_recv) = sems
        self.last = 8 - place.core

    def group(self, way, hop):
        return (self.p.z + NZ - hop + 2 * hop * way) % NZ

    def mine(self, hop):
        return self.all.at[self.group(self.p.core, hop), self.p.y]

    def waits(self, ref, sem):
        self.p.copy(ref, ref, self.o_send.at[0], sem, core=1 - self.p.core).wait_recv()

    def z_copy(self, hop, far):
        p, ref, end = self.p, self.mine(hop), hop + far
        return p.copy(ref, ref, self.z_send.at[end], self.z_recv.at[end],
                      z=(p.z + NZ + far - 2 * far * p.core) % NZ)

    def z_start(self, hop):
        for far in (2, 1):
            @pl.when(hop + far <= self.last)
            def _():
                self.z_copy(hop, far).start()

    def y_copy(self, way, hop):
        p, ref = self.p, self.mine(hop)
        return p.copy(ref, ref, self.y_send.at[way, hop], self.y_recv.at[way, hop],
                      y=(p.y + 1 + 2 * way) % NY)

    def half_copy(self, way, hop):
        p = self.p
        ref = self.half(self.all.at[self.group(p.core, hop), (p.y + 3 + 2 * way) % NY], way)
        return p.copy(ref, ref, self.h_send.at[way, hop], self.h_recv.at[way, hop],
                      y=(p.y + 1 + 2 * way) % NY)

    def sib_copy(self, hop):
        p = self.p
        ref = self.all.at[self.group(p.core, hop)]
        return p.copy(ref, ref, self.s_send.at[hop], self.s_recv.at[hop], core=1 - p.core)

    def own_copy(self, j):
        p = self.p
        ref = self.all.at[p.z, (p.y + 1 + j) % NY]
        return p.copy(ref, ref, self.o_send.at[j], self.o_recv.at[j], core=1 - p.core)

    def begin(self):
        self.z_start(0)

        @pl.when(self.p.core == 0)
        def _():
            self.y_copy(0, 0).start()
            self.y_copy(1, 0).start()

    def there(self, hop):
        return (hop <= self.last) & (hop >= self.p.core)

    def along_z(self, hop):
        @pl.when(hop <= self.last)
        def _():
            self.waits(self.mine(hop), self.z_recv.at[hop])
            self.z_start(hop)
            self.y_copy(0, hop).start()
            self.y_copy(1, hop).start()

        @pl.when(hop - 1 <= self.last)
        def _():
            self.waits(self.mine(hop - 1), self.z_recv.at[hop - 1])
            self.y_copy(0, hop - 1).start()
            self.y_copy(1, hop - 1).start()

    def across_y(self, hop):
        @pl.when(self.there(hop))
        def _():
            for way in range(2):
                self.y_copy(way, hop).wait_recv()
                self.half_copy(way, hop).start()

    def hand_over(self, hop):
        @pl.when(self.there(hop))
        def _():
            for way in range(2):
                self.half_copy(way, hop).wait_recv()

            @pl.when(hop > 0)
            def _():
                self.sib_copy(hop).start()

            @pl.when(hop == 0)
            def _():
                for j in range(3):
                    self.own_copy(j).start()

    def own_arrived(self):
        @pl.when(self.p.core == 1)
        def _():
            for j in range(3):
                self.own_copy(j).wait_recv()

    def sib_arrived(self, hop):
        self.waits(self.all.at[self.group(1 - self.p.core, hop)], self.s_recv.at[hop])

    def settle(self):
        def settle_hop(hop, carry):
            @pl.when((hop > 0) & (hop <= self.last))
            def _():
                self.waits_sent(hop)
                self.sib_copy(hop).wait_send()

            @pl.when(self.there(hop))
            def _():
                for way in range(2):
                    self.y_copy(way, hop).wait_send()
                    self.half_copy(way, hop).wait_send()

            return carry

        lax.fori_loop(0, HOPS, settle_hop, 0)

        @pl.when(self.p.core == 0)
        def _():
            for j in range(3):
                self.own_copy(j).wait_send()

    def waits_sent(self, end):
        self.z_copy(end - 1, 1).wait_send()

    def round(self, m):
        self.along_z(2 * m)
        for hop in (2 * m - 2, 2 * m - 3):
            @pl.when(hop >= 0)
            def _():
                self.across_y(hop)
        for hop in (2 * m - 4, 2 * m - 5):
            @pl.when(hop >= 0)
            def _():
                self.hand_over(hop)


RING_SEMS = [DMA((3,)), DMA((3,)), DMA((HOPS,)), DMA((HOPS,)), DMA((HOPS,)), DMA((HOPS,))]


class Ring:
    def __init__(self, place, everything, part, sems):
        self.p, self.all, self.part = place, everything, part
        self.f_send, self.f_recv, self.z_send, self.z_recv, self.s_send, self.s_recv = sems
        self.last = 8 - place.core

    def group(self, way, step):
        return self.all.at[(self.p.z + NZ - step + 2 * step * way) % NZ, :, self.part]

    def waits(self, ref, sem):
        self.p.copy(ref, ref, self.f_send.at[0], sem, core=1 - self.p.core).wait_recv()

    def first_copy(self, j):
        p, ref = self.p, self.all.at[self.p.z, self.p.y, self.part]
        return p.copy(ref, ref, self.f_send.at[j], self.f_recv.at[j], y=(p.y + 1 + j) % NY)

    def z_copy(self, step):
        p, ref = self.p, self.group(self.p.core, step)
        return p.copy(ref, ref, self.z_send.at[step], self.z_recv.at[step + 1],
                      z=(p.z + 17 - 2 * p.core) % NZ)

    def sib_copy(self, step):
        p, ref = self.p, self.group(self.p.core, step)
        return p.copy(ref, ref, self.s_send.at[step], self.s_recv.at[step], core=1 - p.core)

    def begin(self):
        for j in range(3):
            self.first_copy(j).start()

    def set_off(self):
        for j in range(3):
            self.first_copy(j).wait_recv()
        self.z_copy(0).start()

    def step(self, step):
        @pl.when(step <= self.last)
        def _():
            self.waits(self.group(self.p.core, step), self.z_recv.at[step])

            @pl.when(step < self.last)
            def _():
                self.z_copy(step).start()

            self.sib_copy(step).start()

    def settle(self):
        for j in range(3):
            self.first_copy(j).wait_send()

        def settle_step(step, carry):
            @pl.when(step < self.last)
            def _():
                self.z_copy(step).wait_send()

            @pl.when((step > 0) & (step <= self.last))
            def _():
                self.sib_copy(step).wait_send()

            return carry

        lax.fori_loop(0, HOPS, settle_step, 0)

    def arrived(self):
        def arrival(step, carry):
            @pl.when(step <= 7 + self.p.core)
            def _():
                self.waits(self.group(1 - self.p.core, step), self.s_recv.at[step])

            return carry

        lax.fori_loop(1, HOPS, arrival, 0)


QCOLS = HEADS * HD
PIECE = 16
WIDE = 640


def columns_of(x):
    return (x % 2) * 2 + x // 2


def layer_kernel(
    patch_hbm, q_ref, kv_ref, count_hbm, w_out_hbm, out_ref,
    patch_ref, count_ref, w_out_ref, piece, outgoing, near, onward, landed, q_in, kv_in, queries,
    buf, w, pieces, heads, widen, result, top, acc,
    l_sem, n_send, n_recv, f_send, f_recv, t_send, t_recv, c_send, c_recv,
    wx_send, wx_recv, ax_send, ax_recv, ah_send, ah_recv, r_send, r_recv, *sems,
):
    p = Place()
    keys_values = Spread(p, buf, lambda block, way: block.at[way], sems[:10])
    rings = [Ring(p, w, pl.ds(0, 2), sems[10:16]), Ring(p, w, pl.ds(2, 2), sems[16:])]
    straight = p.xh == p.core
    j_me = p.y * 2 + p.xh
    cut = QCOLS

    def near_device(i):
        return dict(y=i // 2, x=p.core * 2 + p.xl, core=i % 2)

    def near_source(j):
        return dict(y=j // 2, x=(j % 2) * 2 + p.xl, core=p.xh)

    def is_me(i):
        return straight & (p.y * 2 + p.core == i)

    loads = [
        pltpu.make_async_copy(count_hbm, count_ref, l_sem.at[0]),
        pltpu.make_async_copy(patch_hbm, patch_ref, l_sem.at[1]),
        pltpu.make_async_copy(w_out_hbm, w_out_ref, l_sem.at[2]),
    ]
    stays = [
        pltpu.make_async_copy(q_ref, q_in, l_sem.at[3]),
        pltpu.make_async_copy(kv_ref, kv_in, l_sem.at[4]),
    ]
    for load in loads:
        load.start()

    @pl.when(straight)
    def _():
        for load in stays:
            load.start()

    for j in range(8):
        @pl.when(jnp.logical_not(is_me(j)))
        def _():
            p.greet(**near_source(j))
    for i in range(1, NZ):
        p.greet(z=(p.z + i) % NZ)
    for i in range(1, 4):
        p.greet(x=(p.x + i) % 4)
    for i in (1, 2, 3):
        p.greet(y=(p.y + i) % NY)
    p.greet(core=1 - p.core)

    for load in loads:
        load.wait()
    filled = w_out_ref.shape[0]
    row = lax.broadcasted_iota(jnp.int32, (PIECE, filled), 0)
    lane = lax.broadcasted_iota(jnp.int32, (PIECE, filled), 1)
    filling = (row == lane + filled * p.xh).astype(F32).astype(BF)
    for b in range(4):
        piece[b] = jnp.dot(filling, w_out_ref[:, b * QCOLS:(b + 1) * QCOLS],
                           preferred_element_type=F32).astype(BF)

    shards = count_ref.shape[1]
    counts = count_ref[...].astype(F32)
    row = lax.broadcasted_iota(jnp.int32, (shards, shards), 0)
    lane = lax.broadcasted_iota(jnp.int32, (shards, shards), 1)
    ends = jnp.sum(jnp.where(lane <= row, counts, F32(0.0)), axis=1, keepdims=True)
    img_rows = patch_ref.shape[0]
    image = (p.z * 4 + p.y) * 2 + p.xh + shards * lax.broadcasted_iota(
        jnp.int32, (shards, img_rows), 1)
    target = jnp.sum(
        jnp.where(ends <= image.astype(F32), F32(1.0), F32(0.0)), axis=0, keepdims=True
    ).astype(jnp.int32)
    slot = (target & 7) * NZ + (target >> 3)
    mine = (p.z * 4 + p.y) * 2 + p.core
    lane = lax.broadcasted_iota(jnp.int32, (1, shards), 1)
    my_count = jnp.sum(jnp.where(lane == mine, counts, F32(0.0)), axis=1, keepdims=True)
    my_end = jnp.sum(jnp.where(lane <= mine, counts, F32(0.0)), axis=1, keepdims=True)
    local = lax.broadcasted_iota(jnp.int32, (BLK, 1), 0)
    source = jnp.where(
        local >= BLK - my_count.astype(jnp.int32),
        (my_end.astype(jnp.int32) + local - BLK) & (shards - 1), -1
    )
    lane = lax.broadcasted_iota(jnp.int32, (BLK, img_rows), 0)
    placing = (lane == slot).astype(F32).astype(BF)
    outgoing[...] = jnp.dot(placing, patch_ref[...], preferred_element_type=F32).astype(BF)

    pieces[p.x] = piece[columns_of(p.x)]
    depth = NZ * NY * PIECE
    row = lax.broadcasted_iota(jnp.int32, (QCOLS, depth), 0)
    lane = lax.broadcasted_iota(jnp.int32, (QCOLS, depth), 1)
    spot = (lane // PIECE) * (PIECE - 2) + lane % PIECE
    widen[...] = ((row == spot) & (lane % PIECE < PIECE - 2)).astype(F32).astype(BF)
    top[...] = jnp.full_like(top, -1e30)
    acc[...] = jnp.zeros_like(acc)

    @pl.when(straight)
    def _():
        pl.semaphore_wait(pltpu.get_barrier_semaphore(), 29)

    @pl.when(jnp.logical_not(straight))
    def _():
        pl.semaphore_wait(pltpu.get_barrier_semaphore(), 30)

    def near_copy(i):
        return p.copy(outgoing.at[pl.ds(i * NZ, NZ)], near.at[j_me], n_send.at[i], n_recv.at[j_me],
                      **near_device(i))

    def near_arrival(j):
        return p.copy(near.at[j], near.at[j], n_send.at[j], n_recv.at[j], **near_source(j))

    def far_copy(i):
        z = (p.z + i) % NZ
        return p.copy(onward.at[z], landed.at[p.z], f_send.at[i], f_recv.at[p.z], z=z)

    def far_arrival(i):
        z = (p.z + i) % NZ
        return p.copy(landed.at[z], landed.at[z], f_send.at[i], f_recv.at[z], z=z)

    def text_copies():
        to = dict(x=p.core * 2 + p.xl, core=p.xh)
        return (p.copy(q_ref, q_in, t_send.at[0], t_recv.at[0], **to),
                p.copy(kv_ref, kv_in, t_send.at[1], t_recv.at[1], **to))

    def piece_copy(j):
        x = (p.x + j) % 4
        return p.copy(piece.at[columns_of(x)], pieces.at[p.x], wx_send.at[j - 1],
                      wx_recv.at[j - 1], x=x)

    def piece_from(j):
        x = (p.x + 4 - j) % 4
        return p.copy(pieces.at[x], pieces.at[x], wx_send.at[j - 1], wx_recv.at[j - 1], x=x)

    def w_swap(xl):
        ref = w.at[p.z, p.y, 2 * xl + p.core]
        return p.copy(ref, ref, c_send.at[xl], c_recv.at[xl], core=1 - p.core)

    def kv_swap():
        ref = buf.at[p.z, p.y, p.core]
        return p.copy(ref, ref, c_send.at[2], c_recv.at[2], core=1 - p.core)

    for i in range(8):
        @pl.when(jnp.logical_not(is_me(i)))
        def _():
            near_copy(i).start()

        @pl.when(is_me(i))
        def _():
            near[i] = outgoing[i * NZ:(i + 1) * NZ, :]

    @pl.when(jnp.logical_not(straight))
    def _():
        for copy in text_copies():
            copy.start()

    for j in (1, 2, 3):
        piece_copy(j).start()

    for j in range(8):
        @pl.when(jnp.logical_not(is_me(j)))
        def _():
            near_arrival(j).wait_recv()

    held = near[...].reshape(8 * NZ, HEADS * HD + 2 * HD)
    row = lax.broadcasted_iota(jnp.int32, (NZ * 16, 8 * NZ), 0)
    lane = lax.broadcasted_iota(jnp.int32, (NZ * 16, 8 * NZ), 1)
    wanted = (row % 16) // 2 * NZ + row // 16
    second = row % 2 == 1
    zeros = jnp.zeros((8 * NZ, 2 * WIDE - held.shape[1]), BF)
    onward[...] = (
        jnp.dot(((lane == wanted) & jnp.logical_not(second)).astype(F32).astype(BF),
                held[:, :WIDE], preferred_element_type=F32)
        + jnp.dot(((lane == wanted) & second).astype(F32).astype(BF),
                  jnp.concatenate([held[:, WIDE:], zeros], axis=1), preferred_element_type=F32)
    ).astype(BF).reshape(NZ, 16, WIDE)
    order = (8, 7, 9, 6, 10, 5, 11, 4, 12, 3, 13, 2, 14, 1, 15)
    for i in order:
        far_copy(i).start()
    landed[p.z] = onward[p.z]

    for j in (1, 2, 3):
        piece_from(j).wait_recv()
    for xl in range(2):
        w[p.z, p.y, 2 * xl + p.core] = pieces[xl] + pieces[2 + xl]
        w_swap(xl).start()
    for xl in range(2):
        rings[0].waits(w.at[p.z, p.y, 2 * xl + 1 - p.core], c_recv.at[xl])
    for ring in rings:
        ring.begin()

    for ring in rings:
        ring.set_off()

    @pl.when(straight)
    def _():
        for load in stays:
            load.wait()

    @pl.when(jnp.logical_not(straight))
    def _():
        for copy in text_copies():
            copy.wait()

    for i in order:
        far_arrival(i).wait_recv()

    rows = landed[...].reshape(NZ * 16, WIDE)
    lane = lax.broadcasted_iota(jnp.int32, (BLK, NZ * 16), 1)
    first = jnp.dot((lane == source * 2).astype(F32).astype(BF), rows, preferred_element_type=F32)
    rest = jnp.dot((lane == source * 2 + 1).astype(F32).astype(BF), rows, preferred_element_type=F32)
    picked = jnp.concatenate([first, rest[:, :cut + 2 * HD - WIDE]], axis=1)
    is_image = source >= 0
    queries[...] = jnp.where(is_image, picked[:, :cut], q_in[...].astype(F32)).astype(BF)
    buf[p.z, p.y, p.core] = jnp.where(is_image, picked[:, cut:], kv_in[...].astype(F32)).astype(BF)
    kv_swap().start()
    keys_values.waits(buf.at[p.z, p.y, 1 - p.core], c_recv.at[2])
    keys_values.begin()
    for ring in rings:
        ring.step(1)

    def attend(group, masked):
        block = buf[group].reshape(2 * NY * BLK, 2 * HD)
        keys = block[:, :HD]
        values = block[:, HD:]
        values = jnp.concatenate([values, jnp.ones_like(values)], axis=1)
        if masked:
            position = lax.broadcasted_iota(jnp.int32, (BLK, 2 * NY * BLK), 1)
            row = lax.broadcasted_iota(jnp.int32, (BLK, 2 * NY * BLK), 0)
            allowed = position <= (p.y * 2 + p.core) * BLK + row
        for head in range(HEADS):
            rows = pl.ds(head * BLK, BLK)
            scores = lax.dot_general(
                queries[:, head * HD:(head + 1) * HD], keys, NT, preferred_element_type=F32
            ) * SCORE_SCALE
            if masked:
                scores = jnp.where(allowed, scores, F32(-1e30))
            old = top[rows, :]
            new = jnp.maximum(old, jnp.max(scores, axis=1, keepdims=True))
            top[rows, :] = new
            shrink = jnp.exp2(old - new)
            expo = jnp.exp2(scores - new[:, :1]).astype(BF)
            added = jnp.dot(expo, values, preferred_element_type=F32)
            acc[rows, :] = acc[rows, :] * jnp.concatenate([shrink, shrink], axis=1) + added

    def turn(m, carry):
        keys_values.round(m)
        for ring in rings:
            ring.step(m + 1)

        @pl.when(m == 3)
        def _():
            keys_values.own_arrived()
            attend(p.z, True)

        def part(j, carry):
            hop = 2 * m - 4 - j
            way = (p.core + j // 2) % 2
            group = keys_values.group(way, hop)
            here = (hop >= 1) & (hop <= 8 - way)

            @pl.when(here & (j >= 2))
            def _():
                keys_values.sib_arrived(hop)

            @pl.when(here & (group < p.z))
            def _():
                attend(group, False)

            return carry

        lax.fori_loop(0, 4, part, 0)
        return carry

    lax.fori_loop(1, ROUNDS, turn, 0)
    for ring in rings:
        ring.arrived()

    attended = jnp.concatenate(
        [(acc[pl.ds(head * BLK, BLK), :HD] / acc[pl.ds(head * BLK, BLK), HD:]).astype(BF)
         for head in range(HEADS)], axis=1
    )
    heads[p.x] = jnp.dot(attended, widen[...], preferred_element_type=F32).astype(BF)

    def heads_copy(way, j):
        ref = heads.at[p.x, pl.ds((way + j) % 2 * 64, 64)]
        return p.copy(ref, ref, ax_send.at[way, j], ax_recv.at[way, j], x=(p.x + 1 + 2 * way) % 4)

    def heads_half(way):
        ref = heads.at[(p.x + 3 + 2 * way) % 4, pl.ds(way * 64, 64)]
        return p.copy(ref, ref, ah_send.at[way], ah_recv.at[way], x=(p.x + 1 + 2 * way) % 4)

    def product(x):
        rows = w[:, :, columns_of(x)].reshape(depth, QCOLS)
        return jnp.dot(heads[x], rows, preferred_element_type=F32)

    for j in range(2):
        heads_copy(0, j).start()
        heads_copy(1, j).start()
    total = product(p.x)
    for way in range(2):
        heads_copy(way, 0).wait_recv()
        heads_half(way).start()
    for way in range(2):
        heads_copy(way, 1).wait_recv()
    total += product((p.x + 3) % 4)
    total += product((p.x + 1) % 4)
    for way in range(2):
        heads_half(way).wait_recv()
    total += product((p.x + 2) % 4)
    result[...] = total.astype(BF)
    result_copy = p.copy(result, out_ref, r_send, r_recv, x=p.core * 2 + p.xl, core=p.xh)

    @pl.when(straight)
    def _():
        out_ref[...] = result[...]

    @pl.when(jnp.logical_not(straight))
    def _():
        result_copy.start()


    kv_swap().wait_send()
    for xl in range(2):
        w_swap(xl).wait_send()
    for j in (1, 2, 3):
        piece_copy(j).wait_send()
    for way in range(2):
        heads_copy(way, 0).wait_send()
        heads_copy(way, 1).wait_send()
        heads_half(way).wait_send()
    keys_values.settle()
    for ring in rings:
        ring.settle()
    for i in range(8):
        @pl.when(jnp.logical_not(is_me(i)))
        def _():
            near_copy(i).wait_send()
    for i in order:
        far_copy(i).wait_send()

    @pl.when(jnp.logical_not(straight))
    def _():
        result_copy.wait()


def layer(q_text, kv_text, patch_rows, image_count, w_out):
    width = patch_rows.shape[1]
    return pl.pallas_call(
        layer_kernel,
        out_shape=jax.ShapeDtypeStruct((BLK, QCOLS), BF),
        in_specs=[pl.BlockSpec(memory_space=pltpu.HBM)] * 5,
        out_specs=VMEM,
        scratch_shapes=[
            pltpu.VMEM(patch_rows.shape, BF), pltpu.VMEM((1, image_count.shape[0]), jnp.int32),
            pltpu.VMEM(w_out.shape, BF),
            pltpu.VMEM((4, PIECE, QCOLS), BF),
            pltpu.VMEM((BLK, width), BF),
            pltpu.VMEM((8, NZ, width), BF),
            pltpu.VMEM((NZ, 16, WIDE), BF), pltpu.VMEM((NZ, 16, WIDE), BF),
            pltpu.VMEM(q_text.shape, BF), pltpu.VMEM(kv_text.shape, BF),
            pltpu.VMEM(q_text.shape, BF),
            pltpu.VMEM((NZ, NY, 2, BLK, 2 * HD), BF),
            pltpu.VMEM((NZ, NY, 4, PIECE, QCOLS), BF),
            pltpu.VMEM((4, PIECE, QCOLS), BF),
            pltpu.VMEM((4, BLK, NZ * NY * PIECE), BF),
            pltpu.VMEM((QCOLS, NZ * NY * PIECE), BF),
            pltpu.VMEM((BLK, QCOLS), BF),
            pltpu.VMEM((HEADS * BLK, HD), F32),
            pltpu.VMEM((HEADS * BLK, 2 * HD), F32),
            DMA((5,)), DMA((8,)), DMA((8,)), DMA((NZ,)), DMA((NZ,)), DMA((2,)), DMA((2,)),
            DMA((3,)), DMA((3,)),
            DMA((3,)), DMA((3,)), DMA((2, 2)), DMA((2, 2)), DMA((2,)), DMA((2,)), DMA, DMA,
            *SPREAD_SEMS, *RING_SEMS, *RING_SEMS,
        ],
        compiler_params=pltpu.CompilerParams(
            collective_id=0, has_side_effects=True, vmem_limit_bytes=63 * 2**20
        ),
        name="layer",
    )(patch_rows, q_text, kv_text, image_count[None, :], w_out)


def body(q_text, kv_text, patch_rows, image_count, w_out):
    return layer(q_text, kv_text, patch_rows, image_count, w_out)


def solution(mesh):
    in_specs = (P("ctx", "tp"), P("ctx", "tp"), P("ctx", "tp"), P(), P(("tp", "ctx"), None))
    out_specs = P("ctx", "tp")
    return jax.shard_map(body, mesh=mesh, in_specs=in_specs, out_specs=out_specs, check_vma=False)
```
